512 devices in a mesh: blk: 32 (over z_lo, y), dp: 16 (over z_hi, x, core).
Axes of the slice: x: 4, y: 8, z: 8 (z_hi: 2, z_lo: 4; z = z_hi * 4 + z_lo), core: 2. Of those that a mesh axis runs over, the one named last changes fastest.
Arguments:
- queries: bfloat16 [16, 16384, 256], P('dp', 'blk'), may hold values from -8 to 8
- keys: bfloat16 [16, 1024, 256], P('dp', 'blk'), may hold values from -8 to 8
- events: bfloat16 [16, 1024, 4096], P('dp', 'blk'), may hold values from -6 to 6
- value_weight: bfloat16 [4096, 256], P('blk'), may hold values from -0.09375 to 0.09375
- attended_grad: bfloat16 [16, 16384, 256], P('dp', 'blk'), may hold values from -6 to 6
- note_patient: int32 [16, 16384], P('dp', 'blk'), may hold values from 0 to 7, never falling along the last dimension, each value on 1 to 4096 neighbouring positions
- event_patient: int32 [16, 1024], P('dp'), may hold values from 0 to 7, as said below
- block_lists: int32 [16, 128, 2], P('dp', 'blk'), may hold values from 0 to 7, all different within a row
Outputs:
- attended: bfloat16 [16, 16384, 256], P('dp', 'blk')
- query_grad: bfloat16 [16, 16384, 256], P('dp', 'blk')
- key_grad: bfloat16 [16, 1024, 256], P('dp', 'blk')
- event_grad: bfloat16 [16, 1024, 4096], P('dp', 'blk')
- weight_grad: float32 [4096, 256], P('blk')
The draws below stay inside these ranges and needn't reach their ends.
Inputs may be any that keep to these rules, and one draw needn't show every extreme that they name: `note_patient`: patient numbers never fall along a batch's notes. `event_patient`: every aligned block of 128 events holds 16 events of each patient. `block_lists`: the 2 entries of a row name different event blocks; event block n holds events n * 128 to (n + 1) * 128 - 1.
All inputs are finite; a program needn't handle non-finite values.
Results may differ from the reference program's by a relative error of at most 0.03.
Values may be sent and summed in bfloat16 or wider, within the bound.
A program may use at most 64 MiB of HBM per device.

```python
import math
import jax
import jax.numpy as jnp
import numpy as np
from jax import lax

D = 4096
DH = 128
H = 2
BLOCK = 128
KSEL = 2
NPAT = 8
NB = 16
Q = 16384
E = 1024
QB = 128
EB = 8


def draw_queries(key, part):
    key = jax.random.fold_in(key, 11)
    first = jax.random.fold_in(key, 0)
    shape = (NB, Q, H, DH)
    drawn = jnp.clip(jax.random.normal(first, shape, jnp.float32), -4.0, 4.0)
    return drawn.reshape(NB, Q, H * DH).astype(jnp.bfloat16)


def draw_keys(key, part):
    key = jax.random.fold_in(key, 13)
    first = jax.random.fold_in(key, 0)
    shape = (NB, E, H, DH)
    drawn = jnp.clip(jax.random.normal(first, shape, jnp.float32), -4.0, 4.0)
    return drawn.reshape(NB, E, H * DH).astype(jnp.bfloat16)


def draw_event_patient(key, part):
    key = jax.random.fold_in(key, 17)
    block_keys = jax.random.split(key, NB * E // BLOCK)
    orders = jax.vmap(lambda single: jax.random.permutation(single, BLOCK))(block_keys)
    return (orders % NPAT).reshape(NB, E).astype(jnp.int32)


def levels(stream_key, extent, shards, least, high):
    def one(position, shards_of):
        draws = jax.random.uniform(jax.random.fold_in(jax.random.fold_in(stream_key, 6), position), (shards_of,), jnp.float32, least / len(shards), high / len(shards))
        return jnp.repeat(jnp.exp(draws), extent[position] // shards_of).reshape((-1,) + (1,) * (len(extent) - position - 1))

    loudness = one(*shards[0])
    for cut in shards[1:]:
        loudness = loudness * one(*cut)
    return loudness


def distinct(stream_key, rows, count, top, lift):
    sequence = jax.random.permutation(jax.random.fold_in(stream_key, 1), count)
    favour = sequence
    for power in range(3):
        favour = favour * favour // count
    favour = favour * lift // count
    lots = jax.random.randint(jax.random.fold_in(stream_key, 2), (rows, count), 0, 4096) + favour
    fixed_rows = jax.random.permutation(jax.random.fold_in(stream_key, 3), rows)[jnp.arange(count) % rows]
    lots = jnp.where(jnp.arange(rows)[:, None] == fixed_rows[None, :], 1 << 14, lots)
    merit = lots * count + jnp.arange(count)
    return lax.top_k(merit.astype(jnp.int32), top)[1].astype(jnp.int32)


def profile(amount, total, limit, lean):
    weights = [(1 << 20) // math.isqrt(standing ** lean) + 1 for standing in range(2, amount + 1)]
    surplus, counts = total - limit - (amount - 1), [1] * (amount - 1)
    while surplus > 0:
        movable = [i for i in range(amount - 1) if counts[i] < limit]
        mass, left = sum([weights[i] for i in movable]), surplus
        for i in movable:
            addition = min(limit - counts[i], max(1, left * weights[i] // mass), surplus)
            counts[i] = counts[i] + addition
            surplus = surplus - addition
    return np.array([limit] + counts)


def ragged_sizes(rng, number_of, total, bound, lean):
    if number_of == 2:
        one = jax.random.randint(rng, (), max(1, total - bound), min(bound, total - 1) + 1)
        return jnp.stack([one, total - one])
    lengths = jnp.asarray(profile(number_of, total, bound, lean), jnp.int32)
    couples = (number_of - 1) // 2
    donor, sink = lengths[1:1 + 2 * couples:2], lengths[2:2 + 2 * couples:2]
    room = jnp.minimum(donor - 1, bound - sink)
    shifted = jax.random.randint(jax.random.fold_in(rng, 1), (couples,), 0, 1 << 20) % (room + 1)
    lengths = lengths.at[1:1 + 2 * couples:2].set(donor - shifted).at[2:2 + 2 * couples:2].set(sink + shifted)
    return lengths[jax.random.permutation(jax.random.fold_in(rng, 2), number_of)]


def gaussian(stream_key, extent, width, limit, shards=(), kind=jnp.bfloat16):
    result = jax.random.normal(stream_key, extent, jnp.float32) * width
    if len(shards) > 0:
        result = levels(stream_key, extent, shards, -0.22, 0.18) * result
    return jnp.clip(result, min=-limit, max=limit).astype(kind)


def setup_inputs(seed: int = 0) -> dict:
    streams_of = jax.random.split(jax.random.key(seed), 9)
    return {
        "queries": draw_queries(jax.random.fold_in(streams_of[8], 71), 0),
        "keys": draw_keys(jax.random.fold_in(streams_of[8], 71), 0),
        "events": gaussian(streams_of[2], (NB, E, D), 1.0, 6.0, ((0, 16), (1, 32))),
        "value_weight": gaussian(streams_of[3], (D, H * DH), D ** -0.5, 0.09375, ((0, 32),)),
        "attended_grad": gaussian(streams_of[4], (NB, Q, H * DH), 1.0, 6.0, ((0, 16), (1, 32))),
        "note_patient": jax.vmap(lambda own: jnp.searchsorted(jnp.cumsum(ragged_sizes(own, NPAT, Q, 2 * Q // NPAT, 1)), jnp.arange(Q), side="right"))(jax.random.split(streams_of[5], NB)).reshape((NB, Q)).astype(jnp.int32),
        "event_patient": draw_event_patient(jax.random.fold_in(streams_of[8], 71), 0),
        "block_lists": distinct(streams_of[7], NB * QB, EB, KSEL, 4096).reshape((NB, QB, KSEL)),
    }


masked_score = -1e+30

def one_batch(queries, keys, events, value_weight, attended_grad, note_patient, event_patient, block_lists):
    scale = 1.0 / math.sqrt(DH)
    values = jnp.dot(events, value_weight, preferred_element_type=jnp.float32).astype(jnp.bfloat16)
    listed = jnp.any(block_lists[:, :, None] == jnp.arange(EB, dtype=jnp.int32)[None, None, :], axis=1)
    event_block = jnp.arange(E, dtype=jnp.int32) // BLOCK
    key_heads = keys.astype(jnp.float32).reshape(E, H, DH)
    value_heads = values.astype(jnp.float32).reshape(E, H, DH)

    def step(carry, inputs):
        key_sum, value_sum = carry
        query_block, grad_block, patient_block, listed_row = inputs
        allow = listed_row[event_block][None, :] & (patient_block[:, None] == event_patient[None, :])
        query_f = query_block.astype(jnp.float32)
        grad_f = grad_block.astype(jnp.float32)
        score = jnp.einsum('ihd,jhd->hij', query_f, key_heads) * scale
        top = lax.optimization_barrier(jnp.max(jnp.where(allow[None], score, masked_score), axis=2))
        weight = jnp.where(allow[None], jnp.exp(score - top[:, :, None]), 0.0)
        row_sum = lax.optimization_barrier(jnp.sum(weight, axis=2))
        weight_low = lax.optimization_barrier(weight.astype(jnp.bfloat16)).astype(jnp.float32)
        mixed = jnp.einsum('hij,jhd->ihd', weight_low, value_heads) / row_sum.T[:, :, None]
        attended = mixed.astype(jnp.bfloat16)
        log_total = top + jnp.log(row_sum)
        delta = lax.optimization_barrier(jnp.sum(grad_f * attended.astype(jnp.float32), axis=2)).T
        probability = jnp.where(allow[None], jnp.exp(score - log_total[:, :, None]), 0.0)
        prob_grad = jnp.einsum('ihd,jhd->hij', grad_f, value_heads)
        score_grad = probability * (prob_grad - delta[:, :, None])
        score_low = lax.optimization_barrier(score_grad.astype(jnp.bfloat16)).astype(jnp.float32)
        prob_low = lax.optimization_barrier(probability.astype(jnp.bfloat16)).astype(jnp.float32)
        query_grad = (jnp.einsum('hij,jhd->ihd', score_low, key_heads) * scale).astype(jnp.bfloat16)
        key_sum = key_sum + jnp.einsum('hij,ihd->jhd', score_low, query_f)
        value_sum = value_sum + jnp.einsum('hij,ihd->jhd', prob_low, grad_f)
        return ((key_sum, value_sum), (attended, query_grad))
    zeros = jnp.zeros((E, H, DH), jnp.float32)
    inputs = (queries.reshape(QB, BLOCK, H, DH), attended_grad.reshape(QB, BLOCK, H, DH), note_patient.reshape(QB, BLOCK), listed)
    (key_sum, value_sum), (attended, query_grad) = lax.scan(step, (zeros, zeros), inputs)
    key_grad = (key_sum * scale).astype(jnp.bfloat16).reshape(E, H * DH)
    value_low = value_sum.reshape(E, H * DH).astype(jnp.bfloat16)
    event_grad = jnp.dot(value_low, value_weight.T, preferred_element_type=jnp.float32).astype(jnp.bfloat16)
    weight_term = jnp.dot(events.T, value_low, preferred_element_type=jnp.float32)
    return (attended.reshape(Q, H * DH), query_grad.reshape(Q, H * DH), key_grad, event_grad, weight_term)

def reference(queries, keys, events, value_weight, attended_grad, note_patient, event_patient, block_lists):

    def per_batch(inputs):
        return one_batch(inputs[0], inputs[1], inputs[2], value_weight, inputs[3], inputs[4], inputs[5], inputs[6])
    attended, query_grad, key_grad, event_grad, weight_terms = lax.map(per_batch, (queries, keys, events, attended_grad, note_patient, event_patient, block_lists))
    return (attended, query_grad, key_grad, event_grad, lax.optimization_barrier(jnp.sum(weight_terms, axis=0)))
```

```python
import functools
import math

import jax
import jax.numpy as jnp
from jax import lax
from jax.experimental import pallas as pl
from jax.experimental.pallas import tpu as pltpu
from jax.sharding import PartitionSpec as P

MESH = pl.DeviceIdType.MESH
DH = 128
BLOCK = 128
NZ, NY, NX = 4, 8, 4
masked_score = -1e30
scale = 1.0 / math.sqrt(DH)
f32 = jnp.float32
bf16 = jnp.bfloat16

Z_PEERS = [dict(dz=k) for k in (1, 3, 2)]
Y_STEPS = (4, 3, 5, 2, 6, 1, 7)
XC_PEERS = [dict(dx=a, dc=b) for a in (2, 1, 3, 0) for b in (0, 1) if (a, b) != (0, 0)]
ZH_PEERS = [dict(dzh=1, dx=a, dc=b) for a in (2, 1, 3, 0) for b in (0, 1)]


def place():
    blk = lax.axis_index("blk")
    dp = lax.axis_index("dp")
    return blk // NY, blk % NY, dp // 8, (dp // 2) % NX, dp % 2


def device(dz=0, dy=0, dzh=0, dx=0, dc=0):
    z, y, zh, x, c = place()
    return {
        "blk": lax.rem(z + dz, NZ) * NY + lax.rem(y + dy, NY),
        "dp": lax.rem(zh + dzh, 2) * 8 + lax.rem(x + dx, NX) * 2 + lax.rem(c + dc, 2),
    }


class Links:
    def __init__(self, send_sem, recv_sem):
        self.send_sem, self.recv_sem, self.count, self.started = send_sem, recv_sem, 0, []

    def push(self, src, dst, **to):
        index = self.count
        self.count += 1
        copy = pltpu.make_async_remote_copy(
            src_ref=src,
            dst_ref=dst,
            send_sem=self.send_sem.at[index],
            recv_sem=self.recv_sem.at[index],
            device_id=device(**to),
            device_id_type=MESH,
        )
        copy.start()
        self.started.append(copy)
        return copy

    def finish(self):
        for copy in self.started:
            copy.wait_send()


def arrive(copies):
    for copy in copies:
        copy.wait_recv()


def dot(a, b, ca, cb):
    return lax.dot_general(a, b, (((ca,), (cb,)), ((), ())), preferred_element_type=f32)


class Gather:
    def __init__(self, links, buf):
        self.links, self.buf = links, buf
        self.z, self.y = place()[:2]

    def first(self):
        z, y, buf = self.z, self.y, self.buf
        self.a1 = [self.links.push(buf[0].at[z, y], buf[0].at[z, y], **to) for to in Z_PEERS]
        self.b1 = [self.links.push(buf[1].at[z, y], buf[1].at[z, y], dy=k) for k in Y_STEPS]

    def second_a(self):
        arrive(self.a1)
        y, buf = self.y, self.buf
        self.a2 = [self.links.push(buf[0].at[:, y], buf[0].at[:, y], dy=k) for k in Y_STEPS]

    def second_b(self):
        arrive(self.b1)
        z, buf = self.z, self.buf
        self.b2 = [self.links.push(buf[1].at[z], buf[1].at[z], **to) for to in Z_PEERS]

    def done_a(self):
        arrive(self.a2)

    def done_b(self):
        arrive(self.b2)


class Scatter:
    def __init__(self, links, src, ra1, rb1, sa, sb, fa, fb, ra2, rb2):
        self.links, self.src, self.ra1, self.rb1 = links, src, ra1, rb1
        self.sa, self.sb, self.fa, self.fb, self.ra2, self.rb2 = sa, sb, fa, fb, ra2, rb2
        self.z, self.y = place()[:2]

    def first_a(self):
        self.a1 = [
            self.links.push(self.src.at[0, :, lax.rem(self.y + k, NY)], self.ra1.at[k - 1], dy=k)
            for k in Y_STEPS
        ]

    def first_b(self):
        self.b1 = [
            self.links.push(
                self.src.at[1, lax.rem(self.z + to["dz"], NZ)], self.rb1.at[to["dz"] - 1], **to
            )
            for to in Z_PEERS
        ]

    def second_a(self):
        arrive(self.a1)
        total = self.src[0, :, self.y].astype(f32)
        for k in range(NY - 1):
            total = total + self.ra1[k].astype(f32)
        self.fa[...] = total
        self.sa[...] = total.astype(bf16)
        self.a2 = [
            self.links.push(
                self.sa.at[lax.rem(self.z + to["dz"], NZ)], self.ra2.at[to["dz"] - 1], **to
            )
            for to in Z_PEERS
        ]

    def second_b(self):
        arrive(self.b1)
        total = self.src[1, self.z].astype(f32)
        for k in range(NZ - 1):
            total = total + self.rb1[k].astype(f32)
        self.fb[...] = total
        self.sb[...] = total.astype(bf16)
        self.b2 = [
            self.links.push(self.sb.at[lax.rem(self.y + k, NY)], self.rb2.at[k - 1], dy=k)
            for k in Y_STEPS
        ]

    def done_a(self):
        arrive(self.a2)
        total = self.fa[self.z]
        for k in range(NZ - 1):
            total = total + self.ra2[k].astype(f32)
        return total

    def done_b(self):
        arrive(self.b2)
        total = self.fb[self.y]
        for k in range(NY - 1):
            total = total + self.rb2[k].astype(f32)
        return total


def kernel(
    q_ref, k_ref, ev_ref, w_ref, g_ref, np_ref, ep_ref, bl_ref,
    att_ref, qg_ref, kg_ref, eg_ref, wg_ref,
    k0, k1, v0, v1, l0, l1, dvs, dks, wz, evz, pz, rz, ecols, egs, egr,
    ep8, probs, pd, sd, share, shb, sh2, r1, r2,
    va1, vb1, vsa, vsb, vfa, vfb, va2, vb2,
    ka1, kb1, ksa, ksb, kfa, kfb, ka2, kb2,
    send_sem, recv_sem,
):
    kall, vall, lall = (k0, k1), (v0, v1), (l0, l1)
    z, y, zh, x, c = place()
    part = x * 2 + c
    notes = q_ref.shape[1] // BLOCK
    barrier = pltpu.get_barrier_semaphore()
    peers = Z_PEERS + [dict(dy=k) for k in Y_STEPS] + XC_PEERS + ZH_PEERS
    for to in peers:
        pl.semaphore_signal(barrier, inc=1, device_id=device(**to), device_id_type=MESH)
    for h in range(2):
        kall[h][z, y] = k_ref[0, :, h * DH : (h + 1) * DH]
    wz[y] = w_ref[...]
    own_cols = pl.ds(pl.multiple_of(z * 1024, 1024), 1024)
    evz[z] = ev_ref[0, :, own_cols]
    for e in range(8):
        ep8[e : e + 1, :] = ep_ref[:, e * BLOCK : (e + 1) * BLOCK]
    pl.semaphore_wait(barrier, len(peers))

    links = Links(send_sem, recv_sem)
    keys = Gather(links, kall)
    keys.first()
    half = pl.ds(pl.multiple_of(c * 64, 64), 64)
    w1 = [links.push(wz.at[y, half], wz.at[y, half], dy=k) for k in Y_STEPS]
    ev1 = []
    for to in Z_PEERS:
        there = pl.ds(pl.multiple_of(lax.rem(z + to["dz"], NZ) * 1024, 1024), 1024)
        ev1.append(links.push(ev_ref.at[0, :, there], evz.at[z], **to))
    keys.second_a()
    keys.second_b()
    w2 = []
    for k, copy in zip(Y_STEPS, w1):
        copy.wait_recv()
        block = wz.at[lax.rem(y + NY - k, NY), half]
        w2.append(links.push(block, block, dc=1))
    arrive(ev1)
    arrive(w2)
    partial = dot(evz[...].reshape(128, 1024), wz[...].reshape(1024, 256), 1, 0)
    pz[...] = partial.reshape(NZ, 32, 256).astype(bf16)
    z1 = [
        links.push(pz.at[lax.rem(z + to["dz"], NZ)], rz.at[to["dz"] - 1], **to) for to in Z_PEERS
    ]
    spread = []
    for k in Y_STEPS:
        there = pl.ds(pl.multiple_of(lax.rem(y + k, NY) * 128, 128), 128)
        spread.append(links.push(evz.at[:, :, there], ecols.at[:, y], dy=k))
    ecols[:, y] = evz[:, :, pl.ds(pl.multiple_of(y * 128, 128), 128)]

    patients = []
    for n in range(notes):
        row = np_ref[:, n * BLOCK : (n + 1) * BLOCK]
        patients.append(jnp.broadcast_to(row, (BLOCK, BLOCK)).T)

    def chosen(buf, e):
        return buf[e // 2, pl.ds((e % 2) * 4, 4)].reshape(BLOCK, DH)

    def spread_out(dst, h, n, first, second):
        ids = (bl_ref[0, n, 0], bl_ref[0, n, 1])
        none = jnp.zeros_like(first)
        for e in range(8):
            tile = jnp.where(ids[0] == e, first, jnp.where(ids[1] == e, second, none))
            dst[h, n * BLOCK : (n + 1) * BLOCK, e * BLOCK : (e + 1) * BLOCK] = tile

    def head(h):
        return slice(h * DH, (h + 1) * DH)

    def score_head(h):
        for n in range(notes):
            q = q_ref[0, n * BLOCK : (n + 1) * BLOCK, head(h)]
            masked = []
            for slot in range(2):
                e = bl_ref[0, n, slot]
                s = dot(q, chosen(kall[h], e), 1, 1) * scale
                allow = patients[n] == ep8[pl.ds(e, 1), :]
                masked.append(jnp.where(allow, s, masked_score))
            top = jnp.max(jnp.maximum(masked[0], masked[1]), axis=1, keepdims=True)
            weight = [jnp.exp(s - top) for s in masked]
            row_sum = jnp.sum(weight[0] + weight[1], axis=1, keepdims=True)
            inverse = 1.0 / row_sum
            prob = [w * inverse for w in weight]
            for slot in range(2):
                probs[h, n, slot] = prob[slot]
            spread_out(pd, h, n, prob[0].astype(bf16), prob[1].astype(bf16))
        dvs[h] = dot(pd[h], g_ref[0, :, head(h)], 0, 0).astype(bf16).reshape(NZ, NY, 32, DH)

    def value_head(h):
        att = dot(pd[h], vall[h][...].reshape(1024, DH), 1, 0).astype(bf16)
        att_ref[0, :, head(h)] = att
        grad = g_ref[0, :, head(h)]
        delta = jnp.sum(grad.astype(f32) * att.astype(f32), axis=1, keepdims=True)
        for n in range(notes):
            rows = slice(n * BLOCK, (n + 1) * BLOCK)
            low = []
            for slot in range(2):
                pg = dot(grad[rows], chosen(vall[h], bl_ref[0, n, slot]), 1, 1)
                low.append((probs[h, n, slot] * (pg - delta[rows])).astype(bf16))
            spread_out(sd, h, n, low[0], low[1])
        dks[h] = dot(sd[h], q_ref[0, :, head(h)], 0, 0).astype(bf16).reshape(NZ, NY, 32, DH)

    def query_head(h):
        qg = dot(sd[h], kall[h][...].reshape(1024, DH), 1, 0) * scale
        qg_ref[0, :, head(h)] = qg.astype(bf16)

    value_sums = Scatter(links, dvs, va1, vb1, vsa, vsb, vfa, vfb, va2, vb2)
    key_sums = Scatter(links, dks, ka1, kb1, ksa, ksb, kfa, kfb, ka2, kb2)
    keys.done_a()
    score_head(0)
    value_sums.first_a()
    keys.done_b()
    score_head(1)
    value_sums.first_b()

    arrive(z1)
    own = pz[z].astype(f32)
    for k in range(NZ - 1):
        own = own + rz[k].astype(f32)
    for h in range(2):
        vall[h][z, y] = own[:, head(h)].astype(bf16)
    values = Gather(links, vall)
    values.first()
    value_sums.second_a()
    value_sums.second_b()
    values.second_a()
    values.second_b()
    l0[z, y] = value_sums.done_a().astype(bf16)
    l1[z, y] = value_sums.done_b().astype(bf16)
    lows = Gather(links, lall)
    lows.first()
    lows.second_a()
    lows.second_b()
    values.done_a()
    value_head(0)
    key_sums.first_a()
    values.done_b()
    value_head(1)
    key_sums.first_b()
    arrive(spread)
    lows.done_a()
    for h in range(2):
        if h == 1:
            lows.done_b()
        share[:, head(h)] = dot(ecols[...].reshape(1024, 128), lall[h][...].reshape(1024, DH), 0, 0)
    shb[...] = share[...].reshape(8, 16, 256).astype(bf16)
    x1 = []
    for i, to in enumerate(XC_PEERS):
        there = lax.rem(x + to["dx"], NX) * 2 + lax.rem(c + to["dc"], 2)
        x1.append(links.push(shb.at[there], r1.at[i], **to))
    low_rows = jnp.concatenate([lall[h][:, y].reshape(128, DH) for h in range(2)], axis=1)
    egs[...] = dot(low_rows, wz[...].reshape(1024, 256), 1, 1).astype(bf16).reshape(NZ, 32, 1024)
    e1 = [
        links.push(egs.at[lax.rem(z + to["dz"], NZ)], egr.at[z], **to) for to in Z_PEERS
    ]
    egr[z] = egs[z]
    arrive(x1)
    total = shb[part].astype(f32)
    for i in range(7):
        total = total + r1[i].astype(f32)
    sh2[...] = total.astype(bf16)
    x2 = [links.push(sh2, r2.at[zh, part], **to) for to in XC_PEERS + ZH_PEERS]
    r2[zh, part] = sh2[...]
    for h in range(2):
        query_head(h)
    key_sums.second_a()
    key_sums.second_b()
    arrive(e1)
    for k in range(NZ):
        eg_ref[0, :, k * 1024 : (k + 1) * 1024] = egr[k]
    kg_ref[0, :, head(0)] = (key_sums.done_a() * scale).astype(bf16)
    kg_ref[0, :, head(1)] = (key_sums.done_b() * scale).astype(bf16)
    arrive(x2)
    wg_ref[...] = (r2[0].astype(f32) + r2[1].astype(f32)).reshape(128, 256)
    links.finish()


def scatter_scratch():
    return [
        pltpu.VMEM((NY - 1, NZ, 32, DH), bf16),
        pltpu.VMEM((NZ - 1, NY, 32, DH), bf16),
        pltpu.VMEM((NZ, 32, DH), bf16),
        pltpu.VMEM((NY, 32, DH), bf16),
        pltpu.VMEM((NZ, 32, DH), f32),
        pltpu.VMEM((NY, 32, DH), f32),
        pltpu.VMEM((NZ - 1, 32, DH), bf16),
        pltpu.VMEM((NY - 1, 32, DH), bf16),
    ]


def shards(*args):
    def shape(s, t):
        return jax.ShapeDtypeStruct(s, t)

    vmem = pl.BlockSpec(memory_space=pltpu.VMEM)
    pair = pltpu.VMEM((2, NZ, NY, 32, DH), bf16)
    single = pltpu.VMEM((NZ, NY, 32, DH), bf16)
    return pl.pallas_call(
        kernel,
        out_shape=(
            shape((1, 512, 256), bf16),
            shape((1, 512, 256), bf16),
            shape((1, 32, 256), bf16),
            shape((1, 32, 4096), bf16),
            shape((128, 256), f32),
        ),
        in_specs=[vmem] * 7 + [pl.BlockSpec(memory_space=pltpu.SMEM)],
        out_specs=(vmem,) * 5,
        scratch_shapes=[single] * 6
        + [pair] * 2
        + [
            pltpu.VMEM((NY, 128, 256), bf16),
            pltpu.VMEM((NZ, 32, 1024), bf16),
            pltpu.VMEM((NZ, 32, 256), bf16),
            pltpu.VMEM((NZ - 1, 32, 256), bf16),
            pltpu.VMEM((NZ, NY, 32, 128), bf16),
            pltpu.VMEM((NZ, 32, 1024), bf16),
            pltpu.VMEM((NZ, 32, 1024), bf16),
            pltpu.VMEM((8, BLOCK), jnp.int32),
            pltpu.VMEM((2, 4, 2, BLOCK, BLOCK), f32),
            pltpu.VMEM((2, 512, 1024), bf16),
            pltpu.VMEM((2, 512, 1024), bf16),
            pltpu.VMEM((128, 256), f32),
            pltpu.VMEM((8, 16, 256), bf16),
            pltpu.VMEM((16, 256), bf16),
            pltpu.VMEM((7, 16, 256), bf16),
            pltpu.VMEM((2, 8, 16, 256), bf16),
        ]
        + scatter_scratch()
        + scatter_scratch()
        + [pltpu.SemaphoreType.DMA((160,)), pltpu.SemaphoreType.DMA((160,))],
        compiler_params=pltpu.CompilerParams(
            collective_id=0, has_side_effects=True, vmem_limit_bytes=40 * 1024 * 1024
        ),
        name="notes",
    )(*args)


def solution(mesh):
    return jax.shard_map(
        shards,
        mesh=mesh,
        in_specs=(
            P("dp", "blk", None),
            P("dp", "blk", None),
            P("dp", "blk", None),
            P("blk", None),
            P("dp", "blk", None),
            P("dp", "blk"),
            P("dp", None),
            P("dp", "blk", None),
        ),
        out_specs=(
            P("dp", "blk", None),
            P("dp", "blk", None),
            P("dp", "blk", None),
            P("dp", "blk", None),
            P("blk", None),
        ),
        check_vma=False,
    )
```

```python
import functools
import math

import jax
import jax.numpy as jnp
from jax import lax
from jax.experimental import pallas as pl
from jax.experimental.pallas import tpu as pltpu
from jax.sharding import PartitionSpec as P

MESH = pl.DeviceIdType.MESH
DH = 128
BLOCK = 128
NZ, NY, NX = 4, 8, 4
masked_score = -1e30
scale = 1.0 / math.sqrt(DH)
f32 = jnp.float32
bf16 = jnp.bfloat16

Z_PEERS = [dict(dz=k) for k in (1, 3, 2)]
Y_STEPS = (4, 3, 5, 2, 6, 1, 7)
XC_PEERS = [dict(dx=a, dc=b) for a in (2, 1, 3, 0) for b in (0, 1) if (a, b) != (0, 0)]
ZH_PEERS = [dict(dzh=1, dx=a, dc=b) for a in (2, 1, 3, 0) for b in (0, 1)]


def place():
    blk = lax.axis_index("blk")
    dp = lax.axis_index("dp")
    return blk // NY, blk % NY, dp // 8, (dp // 2) % NX, dp % 2


def device(dz=0, dy=0, dzh=0, dx=0, dc=0):
    z, y, zh, x, c = place()
    return {
        "blk": lax.rem(z + dz, NZ) * NY + lax.rem(y + dy, NY),
        "dp": lax.rem(zh + dzh, 2) * 8 + lax.rem(x + dx, NX) * 2 + lax.rem(c + dc, 2),
    }


class Links:
    def __init__(self, send_sem, recv_sem):
        self.send_sem, self.recv_sem, self.count, self.started = send_sem, recv_sem, 0, []

    def push(self, src, dst, **to):
        index = self.count
        self.count += 1
        copy = pltpu.make_async_remote_copy(
            src_ref=src,
            dst_ref=dst,
            send_sem=self.send_sem.at[index],
            recv_sem=self.recv_sem.at[index],
            device_id=device(**to),
            device_id_type=MESH,
        )
        copy.start()
        self.started.append(copy)
        return copy

    def fetch(self, src, dst, sem):
        copy = pltpu.make_async_copy(src, dst, sem)
        copy.start()
        return copy

    def finish(self):
        for copy in self.started:
            copy.wait_send()


def arrive(copies):
    for copy in copies:
        copy.wait_recv()


def dot(a, b, ca, cb):
    return lax.dot_general(a, b, (((ca,), (cb,)), ((), ())), preferred_element_type=f32)


class Gather:
    def __init__(self, links, buf):
        self.links, self.buf = links, buf
        self.z, self.y = place()[:2]

    def first(self):
        z, y, buf = self.z, self.y, self.buf
        self.a1 = [self.links.push(buf[0].at[z, y], buf[0].at[z, y], **to) for to in Z_PEERS]
        self.b1 = [self.links.push(buf[1].at[z, y], buf[1].at[z, y], dy=k) for k in Y_STEPS]

    def second_a(self):
        arrive(self.a1)
        y, buf = self.y, self.buf
        self.a2 = [self.links.push(buf[0].at[:, y], buf[0].at[:, y], dy=k) for k in Y_STEPS]

    def second_b(self):
        arrive(self.b1)
        z, buf = self.z, self.buf
        self.b2 = [self.links.push(buf[1].at[z], buf[1].at[z], **to) for to in Z_PEERS]

    def done_a(self):
        arrive(self.a2)

    def done_b(self):
        arrive(self.b2)


class Scatter:
    def __init__(self, links, src, ra1, rb1, sa, sb, fa, fb, ra2, rb2):
        self.links, self.src, self.ra1, self.rb1 = links, src, ra1, rb1
        self.sa, self.sb, self.fa, self.fb, self.ra2, self.rb2 = sa, sb, fa, fb, ra2, rb2
        self.z, self.y = place()[:2]

    def first_a(self):
        self.a1 = [
            self.links.push(self.src.at[0, :, lax.rem(self.y + k, NY)], self.ra1.at[k - 1], dy=k)
            for k in Y_STEPS
        ]

    def first_b(self):
        self.b1 = [
            self.links.push(
                self.src.at[1, lax.rem(self.z + to["dz"], NZ)], self.rb1.at[to["dz"] - 1], **to
            )
            for to in Z_PEERS
        ]

    def second_a(self):
        arrive(self.a1)
        total = self.src[0, :, self.y].astype(f32)
        for k in range(NY - 1):
            total = total + self.ra1[k].astype(f32)
        self.fa[...] = total
        self.sa[...] = total.astype(bf16)
        self.a2 = [
            self.links.push(
                self.sa.at[lax.rem(self.z + to["dz"], NZ)], self.ra2.at[to["dz"] - 1], **to
            )
            for to in Z_PEERS
        ]

    def second_b(self):
        arrive(self.b1)
        total = self.src[1, self.z].astype(f32)
        for k in range(NZ - 1):
            total = total + self.rb1[k].astype(f32)
        self.fb[...] = total
        self.sb[...] = total.astype(bf16)
        self.b2 = [
            self.links.push(self.sb.at[lax.rem(self.y + k, NY)], self.rb2.at[k - 1], dy=k)
            for k in Y_STEPS
        ]

    def done_a(self):
        arrive(self.a2)
        total = self.fa[self.z]
        for k in range(NZ - 1):
            total = total + self.ra2[k].astype(f32)
        return total

    def done_b(self):
        arrive(self.b2)
        total = self.fb[self.y]
        for k in range(NY - 1):
            total = total + self.rb2[k].astype(f32)
        return total


def kernel(
    q_in, k_in, ev_in, w_in, g_in, np_in, ep_in, bl_in,
    att_ref, qg_ref, kg_ref, eg_ref, wg_ref,
    k0, k1, v0, v1, dvs, dks, wz, evz, pz, rz, egs, egr,
    ep8, probs, pd, sd, lz0, lz1, pw, pr, xs, xr, ys, yr, sh2, r2,
    va1, vb1, vsa, vsb, vfa, vfb, va2, vb2,
    ka1, kb1, ksa, ksb, kfa, kfb, ka2, kb2,
    q_ref, ev_ref, g_ref, np_ref, ep_ref, bl_ref, in_sem, send_sem, recv_sem,
):
    kall, vall = (k0, k1), (v0, v1)
    z, y, zh, x, c = place()
    part = x * 2 + c
    notes = q_ref.shape[1] // BLOCK
    barrier = pltpu.get_barrier_semaphore()
    peers = Z_PEERS + [dict(dy=k) for k in Y_STEPS] + XC_PEERS + ZH_PEERS
    for to in peers:
        pl.semaphore_signal(barrier, inc=1, device_id=device(**to), device_id_type=MESH)
    links = Links(send_sem, recv_sem)
    own_cols = pl.ds(pl.multiple_of(z * 1024, 1024), 1024)
    loads = [
        links.fetch(src, dst, in_sem.at[i])
        for i, (src, dst) in enumerate(
            [
                (k_in.at[0, :, :DH], k0.at[z, y]),
                (k_in.at[0, :, DH:], k1.at[z, y]),
                (w_in, wz.at[y]),
                (ev_in, ev_ref),
                (ev_in.at[0, :, own_cols], evz.at[z]),
                (q_in, q_ref),
                (g_in, g_ref),
                (np_in, np_ref),
                (ep_in, ep_ref),
                (bl_in, bl_ref),
            ]
        )
    ]
    pl.semaphore_wait(barrier, len(peers))
    for load in loads[:2]:
        load.wait()
    keys = Gather(links, kall)
    keys.first()
    for load in loads[2:4]:
        load.wait()
    half = pl.ds(pl.multiple_of(c * 64, 64), 64)
    w1 = [links.push(wz.at[y, half], wz.at[y, half], dy=k) for k in Y_STEPS]
    ev1 = []
    for to in Z_PEERS:
        there = pl.ds(pl.multiple_of(lax.rem(z + to["dz"], NZ) * 1024, 1024), 1024)
        ev1.append(links.push(ev_ref.at[0, :, there], evz.at[z], **to))
    for load in loads[4:]:
        load.wait()
    for e in range(8):
        ep8[e : e + 1, :] = ep_ref[:, e * BLOCK : (e + 1) * BLOCK]
    keys.second_a()
    keys.second_b()
    w2 = []
    for k, copy in zip(Y_STEPS, w1):
        copy.wait_recv()
        block = wz.at[lax.rem(y + NY - k, NY), half]
        w2.append(links.push(block, block, dc=1))
    arrive(ev1)
    arrive(w2)
    partial = dot(evz[...].reshape(128, 1024), wz[...].reshape(1024, 256), 1, 0)
    pz[...] = partial.reshape(NZ, 32, 256).astype(bf16)
    z1 = [
        links.push(pz.at[lax.rem(z + to["dz"], NZ)], rz.at[to["dz"] - 1], **to) for to in Z_PEERS
    ]
    patients = []
    for n in range(notes):
        row = np_ref[:, n * BLOCK : (n + 1) * BLOCK]
        patients.append(jnp.broadcast_to(row, (BLOCK, BLOCK)).T)

    def chosen(buf, e):
        return buf[e // 2, pl.ds((e % 2) * 4, 4)].reshape(BLOCK, DH)

    def spread_out(dst, h, n, first, second):
        ids = (bl_ref[0, 0, n], bl_ref[0, 1, n])
        none = jnp.zeros_like(first)
        for e in range(8):
            tile = jnp.where(ids[0] == e, first, jnp.where(ids[1] == e, second, none))
            dst[h, n * BLOCK : (n + 1) * BLOCK, e * BLOCK : (e + 1) * BLOCK] = tile

    def head(h):
        return slice(h * DH, (h + 1) * DH)

    def score_head(h):
        for n in range(notes):
            q = q_ref[0, n * BLOCK : (n + 1) * BLOCK, head(h)]
            masked = []
            for slot in range(2):
                e = bl_ref[0, slot, n]
                s = dot(q, chosen(kall[h], e), 1, 1) * scale
                allow = patients[n] == ep8[pl.ds(e, 1), :]
                masked.append(jnp.where(allow, s, masked_score))
            top = jnp.max(jnp.maximum(masked[0], masked[1]), axis=1, keepdims=True)
            weight = [jnp.exp(s - top) for s in masked]
            row_sum = jnp.sum(weight[0] + weight[1], axis=1, keepdims=True)
            inverse = 1.0 / row_sum
            prob = [w * inverse for w in weight]
            for slot in range(2):
                probs[h, n, slot] = prob[slot]
            spread_out(pd, h, n, prob[0].astype(bf16), prob[1].astype(bf16))
        dvs[h] = dot(pd[h], g_ref[0, :, head(h)], 0, 0).astype(bf16).reshape(NZ, NY, 32, DH)

    def value_head(h):
        att = dot(pd[h], vall[h][...].reshape(1024, DH), 1, 0).astype(bf16)
        att_ref[0, :, head(h)] = att
        grad = g_ref[0, :, head(h)]
        delta = jnp.sum(grad.astype(f32) * att.astype(f32), axis=1, keepdims=True)
        for n in range(notes):
            rows = slice(n * BLOCK, (n + 1) * BLOCK)
            low = []
            for slot in range(2):
                pg = dot(grad[rows], chosen(vall[h], bl_ref[0, slot, n]), 1, 1)
                low.append((probs[h, n, slot] * (pg - delta[rows])).astype(bf16))
            spread_out(sd, h, n, low[0], low[1])
        dks[h] = dot(sd[h], q_ref[0, :, head(h)], 0, 0).astype(bf16).reshape(NZ, NY, 32, DH)

    def query_head(h):
        qg = dot(sd[h], kall[h][...].reshape(1024, DH), 1, 0) * scale
        qg_ref[0, :, head(h)] = qg.astype(bf16)
    value_sums = Scatter(links, dvs, va1, vb1, vsa, vsb, vfa, vfb, va2, vb2)
    key_sums = Scatter(links, dks, ka1, kb1, ksa, ksb, kfa, kfb, ka2, kb2)
    keys.done_a()
    score_head(0)
    value_sums.first_a()
    keys.done_b()
    score_head(1)
    value_sums.first_b()
    arrive(z1)
    own = pz[z].astype(f32)
    for k in range(NZ - 1):
        own = own + rz[k].astype(f32)
    for h in range(2):
        vall[h][z, y] = own[:, head(h)].astype(bf16)
    values = Gather(links, vall)
    values.first()
    value_sums.second_a()
    value_sums.second_b()
    values.second_a()
    values.second_b()
    lz0[z] = value_sums.done_a().astype(bf16)
    low1 = []
    low1 += [links.push(lz0.at[z], lz0.at[z], **to) for to in Z_PEERS]
    lz1[z] = value_sums.done_b().astype(bf16)
    low1 += [links.push(lz1.at[z], lz1.at[z], **to) for to in Z_PEERS]
    values.done_a()
    value_head(0)
    key_sums.first_a()
    arrive(low1)
    low_rows = jnp.concatenate([lz0[...].reshape(128, DH), lz1[...].reshape(128, DH)], axis=1)
    c1 = []
    for k in range(NY):
        cols = evz[:, :, k * 128 : (k + 1) * 128].reshape(128, 128)
        pw[k] = dot(cols, low_rows, 0, 0).astype(bf16).reshape(NX, 2, 16, 256)
        c1.append(links.push(pw.at[k, :, 1 - c], pr.at[k], dc=1))
    values.done_b()
    value_head(1)
    key_sums.first_b()
    for k in range(NY):
        c1[k].wait_recv()
        xs[k] = (pw[k, :, c].astype(f32) + pr[k].astype(f32)).astype(bf16)
    x1 = [links.push(xs.at[:, lax.rem(x + k, NX)], xr.at[k - 1], dx=k) for k in (2, 1, 3)]
    arrive(x1)
    total = xs[:, x].astype(f32)
    for k in range(NX - 1):
        total = total + xr[k].astype(f32)
    ys[...] = total.astype(bf16)
    y1 = [links.push(ys.at[lax.rem(y + k, NY)], yr.at[k - 1], dy=k) for k in Y_STEPS]
    egs[...] = dot(low_rows, wz[...].reshape(1024, 256), 1, 1).astype(bf16).reshape(NZ, 32, 1024)
    e1 = [
        links.push(egs.at[lax.rem(z + to["dz"], NZ)], egr.at[z], **to) for to in Z_PEERS
    ]
    egr[z] = egs[z]
    arrive(y1)
    total = ys[y].astype(f32)
    for k in range(NY - 1):
        total = total + yr[k].astype(f32)
    sh2[...] = total.astype(bf16)
    x2 = [links.push(sh2, r2.at[zh, part], **to) for to in XC_PEERS + ZH_PEERS]
    r2[zh, part] = sh2[...]
    for h in range(2):
        query_head(h)
    key_sums.second_a()
    key_sums.second_b()
    arrive(e1)
    for k in range(NZ):
        eg_ref[0, :, k * 1024 : (k + 1) * 1024] = egr[k]
    kg_ref[0, :, head(0)] = (key_sums.done_a() * scale).astype(bf16)
    kg_ref[0, :, head(1)] = (key_sums.done_b() * scale).astype(bf16)
    arrive(x2)
    wg_ref[...] = (r2[0].astype(f32) + r2[1].astype(f32)).reshape(128, 256)
    links.finish()


def scatter_scratch():
    return [
        pltpu.VMEM((NY - 1, NZ, 32, DH), bf16),
        pltpu.VMEM((NZ - 1, NY, 32, DH), bf16),
        pltpu.VMEM((NZ, 32, DH), bf16),
        pltpu.VMEM((NY, 32, DH), bf16),
        pltpu.VMEM((NZ, 32, DH), f32),
        pltpu.VMEM((NY, 32, DH), f32),
        pltpu.VMEM((NZ - 1, 32, DH), bf16),
        pltpu.VMEM((NY - 1, 32, DH), bf16),
    ]


def hand_over(*refs):
    for i in range(5):
        refs[5 + i][...] = refs[i][...]


def shards(*args):
    def shape(s, t):
        return jax.ShapeDtypeStruct(s, t)

    vmem = pl.BlockSpec(memory_space=pltpu.VMEM)
    pair = pltpu.VMEM((2, NZ, NY, 32, DH), bf16)
    single = pltpu.VMEM((NZ, NY, 32, DH), bf16)
    results = pl.pallas_call(
        kernel,
        out_shape=(
            shape((1, 512, 256), bf16),
            shape((1, 512, 256), bf16),
            shape((1, 32, 256), bf16),
            shape((1, 32, 4096), bf16),
            shape((128, 256), f32),
        ),
        in_specs=[pl.BlockSpec(memory_space=pl.ANY)] * 8,
        out_specs=(vmem,) * 5,
        scratch_shapes=[single] * 4
        + [pair] * 2
        + [
            pltpu.VMEM((NY, 128, 256), bf16),
            pltpu.VMEM((NZ, 32, 1024), bf16),
            pltpu.VMEM((NZ, 32, 256), bf16),
            pltpu.VMEM((NZ - 1, 32, 256), bf16),
            pltpu.VMEM((NZ, 32, 1024), bf16),
            pltpu.VMEM((NZ, 32, 1024), bf16),
            pltpu.VMEM((8, BLOCK), jnp.int32),
            pltpu.VMEM((2, 4, 2, BLOCK, BLOCK), f32),
            pltpu.VMEM((2, 512, 1024), bf16),
            pltpu.VMEM((2, 512, 1024), bf16),
            pltpu.VMEM((NZ, 32, DH), bf16),
            pltpu.VMEM((NZ, 32, DH), bf16),
            pltpu.VMEM((NY, NX, 2, 16, 256), bf16),
            pltpu.VMEM((NY, NX, 16, 256), bf16),
            pltpu.VMEM((NY, NX, 16, 256), bf16),
            pltpu.VMEM((NX - 1, NY, 16, 256), bf16),
            pltpu.VMEM((NY, 16, 256), bf16),
            pltpu.VMEM((NY - 1, 16, 256), bf16),
            pltpu.VMEM((16, 256), bf16),
            pltpu.VMEM((2, 8, 16, 256), bf16),
        ]
        + scatter_scratch()
        + scatter_scratch()
        + [
            pltpu.VMEM((1, 512, 256), bf16),
            pltpu.VMEM((1, 32, 4096), bf16),
            pltpu.VMEM((1, 512, 256), bf16),
            pltpu.VMEM((1, 512), jnp.int32),
            pltpu.VMEM((1, 1024), jnp.int32),
            pltpu.SMEM((1, 2, 4), jnp.int32),
            pltpu.SemaphoreType.DMA((10,)),
        ]
        + [pltpu.SemaphoreType.DMA((160,)), pltpu.SemaphoreType.DMA((160,))],
        compiler_params=pltpu.CompilerParams(
            collective_id=0, has_side_effects=True, vmem_limit_bytes=60 * 1024 * 1024
        ),
        name="notes",
    )(*args[:7], jnp.swapaxes(args[7], 1, 2))
    return pl.pallas_call(
        hand_over,
        out_shape=tuple(shape(r.shape, r.dtype) for r in results),
        name="hand_over",
    )(*results)


def solution(mesh):
    return jax.shard_map(
        shards,
        mesh=mesh,
        in_specs=(
            P("dp", "blk", None),
            P("dp", "blk", None),
            P("dp", "blk", None),
            P("blk", None),
            P("dp", "blk", None),
            P("dp", "blk"),
            P("dp", None),
            P("dp", "blk", None),
        ),
        out_specs=(
            P("dp", "blk", None),
            P("dp", "blk", None),
            P("dp", "blk", None),
            P("dp", "blk", None),
            P("blk", None),
        ),
        check_vma=False,
    )
```

```python
import functools
import math

import jax
import jax.numpy as jnp
from jax import lax
from jax.experimental import pallas as pl
from jax.experimental.pallas import tpu as pltpu
from jax.sharding import PartitionSpec as P

MESH = pl.DeviceIdType.MESH
DH = 128
BLOCK = 128
NZ, NY, NX = 4, 8, 4
masked_score = -1e30
scale = 1.0 / math.sqrt(DH)
f32 = jnp.float32
bf16 = jnp.bfloat16

Z_PEERS = [dict(dz=k) for k in (1, 3, 2)]
Y_STEPS = (4, 3, 5, 2, 6, 1, 7)
XC_PEERS = [dict(dx=a, dc=b) for a in (2, 1, 3, 0) for b in (0, 1) if (a, b) != (0, 0)]
ZH_PEERS = [dict(dzh=1)]


def place():
    blk = lax.axis_index("blk")
    dp = lax.axis_index("dp")
    return blk // NY, blk % NY, dp // 8, (dp // 2) % NX, dp % 2


def device(dz=0, dy=0, dzh=0, dx=0, dc=0):
    z, y, zh, x, c = place()
    return {
        "blk": lax.rem(z + dz, NZ) * NY + lax.rem(y + dy, NY),
        "dp": lax.rem(zh + dzh, 2) * 8 + lax.rem(x + dx, NX) * 2 + lax.rem(c + dc, 2),
    }


class Links:
    def __init__(self, send_sem, recv_sem):
        self.send_sem, self.recv_sem, self.count, self.started = send_sem, recv_sem, 0, []

    def push(self, src, dst, **to):
        index = self.count
        self.count += 1
        copy = pltpu.make_async_remote_copy(
            src_ref=src,
            dst_ref=dst,
            send_sem=self.send_sem.at[index],
            recv_sem=self.recv_sem.at[index],
            device_id=device(**to),
            device_id_type=MESH,
        )
        copy.start()
        self.started.append(copy)
        return copy

    def fetch(self, src, dst, sem):
        copy = pltpu.make_async_copy(src, dst, sem)
        copy.start()
        return copy

    def finish(self):
        for copy in self.started:
            copy.wait_send()


def arrive(copies):
    for copy in copies:
        copy.wait_recv()


def dot(a, b, ca, cb):
    return lax.dot_general(a, b, (((ca,), (cb,)), ((), ())), preferred_element_type=f32)


class Gather:
    def __init__(self, links, buf):
        self.links, self.buf = links, buf
        self.z, self.y = place()[:2]

    def first_a(self):
        z, y, buf = self.z, self.y, self.buf
        self.a1 = [self.links.push(buf[0].at[z, y], buf[0].at[z, y], **to) for to in Z_PEERS]

    def first_b(self):
        z, y, buf = self.z, self.y, self.buf
        self.b1 = [self.links.push(buf[1].at[z, y], buf[1].at[z, y], dy=k) for k in Y_STEPS]

    def second_a(self):
        y, buf = self.y, self.buf
        self.a2 = [self.links.push(buf[0].at[:, y], buf[0].at[:, y], dy=k) for k in Y_STEPS]

    def second_b(self):
        arrive(self.b1)
        z, buf = self.z, self.buf
        self.b2 = [self.links.push(buf[1].at[z], buf[1].at[z], **to) for to in Z_PEERS]

    def done_a(self):
        arrive(self.a2)

    def done_b(self):
        arrive(self.b2)


class Scatter:
    def __init__(self, links, src, ra1, rb1, sa, sb, fa, fb, ra2, rb2):
        self.links, self.src, self.ra1, self.rb1 = links, src, ra1, rb1
        self.sa, self.sb, self.fa, self.fb, self.ra2, self.rb2 = sa, sb, fa, fb, ra2, rb2
        self.z, self.y = place()[:2]

    def first_a(self):
        self.a1 = [
            self.links.push(self.src.at[0, :, lax.rem(self.y + k, NY)], self.ra1.at[k - 1], dy=k)
            for k in Y_STEPS
        ]

    def first_b(self):
        self.b1 = [
            self.links.push(
                self.src.at[1, lax.rem(self.z + to["dz"], NZ)], self.rb1.at[to["dz"] - 1], **to
            )
            for to in Z_PEERS
        ]

    def second_a(self, whole=False):
        arrive(self.a1)
        total = self.src[0, :, self.y].astype(f32)
        for k in range(NY - 1):
            total = total + self.ra1[k].astype(f32)
        self.fa[...] = total
        self.sa[...] = total.astype(bf16)
        self.a2 = [
            self.links.push(
                self.sa if whole else self.sa.at[lax.rem(self.z + to["dz"], NZ)],
                self.ra2.at[to["dz"] - 1],
                **to,
            )
            for to in Z_PEERS
        ]

    def second_b(self):
        arrive(self.b1)
        total = self.src[1, self.z].astype(f32)
        for k in range(NZ - 1):
            total = total + self.rb1[k].astype(f32)
        self.fb[...] = total
        self.sb[...] = total.astype(bf16)
        self.b2 = [
            self.links.push(self.sb.at[lax.rem(self.y + k, NY)], self.rb2.at[k - 1], dy=k)
            for k in Y_STEPS
        ]

    def done_a(self, whole=False):
        arrive(self.a2)
        total = self.fa[...] if whole else self.fa[self.z]
        for k in range(NZ - 1):
            total = total + self.ra2[k].astype(f32)
        return total

    def done_b(self):
        arrive(self.b2)
        total = self.fb[self.y]
        for k in range(NY - 1):
            total = total + self.rb2[k].astype(f32)
        return total


def kernel(
    q_in, k_in, ev_in, w_in, g_in, np_in, ep_in, bl_in,
    att_out, qg_out, kg_out, eg_out, wg_out,
    k0, k1, v0, v1, dvs, dks, wq, wz, evz, pz0, pz1, rz0, rz1, evt, egs, egr,
    ep8, probs, pd, sd, lz0, lz1, pw, pr, xs, xr, ys, yr, sh2, rzh, sh3, r2,
    va1, vb1, vsa, vsb, vfa, vfb, va2, vb2,
    ka1, kb1, ksa, ksb, kfa, kfb, ka2, kb2,
    q_ref, ev_ref, g_ref, np_ref, ep_ref, bl_ref, att_ref, qg_ref, kg_ref, in_sem, out_sem, send_sem, recv_sem,
):
    kall, vall = (k0, k1), (v0, v1)
    z, y, zh, x, c = place()
    part = x * 2 + c
    notes = q_ref.shape[1] // BLOCK
    barrier = pltpu.get_barrier_semaphore()
    peers = ZH_PEERS + [dict(dy=k) for k in Y_STEPS] + Z_PEERS + XC_PEERS
    for to in peers:
        pl.semaphore_signal(barrier, inc=1, device_id=device(**to), device_id_type=MESH)
    links = Links(send_sem, recv_sem)
    own_cols = pl.ds(pl.multiple_of(z * 1024, 1024), 1024)
    loads = [
        links.fetch(src, dst, in_sem.at[i])
        for i, (src, dst) in enumerate(
            [
                (k_in.at[0, :, :DH], k0.at[z, y]),
                (k_in.at[0, :, DH:], k1.at[z, y]),
                (w_in.at[pl.ds(pl.multiple_of(part * 16, 16), 16)], wq.at[x, c, y]),
                (ev_in, ev_ref),
                (ev_in.at[0, :, own_cols], evz.at[z]),
                (q_in, q_ref),
                (g_in, g_ref),
                (np_in, np_ref),
                (ep_in, ep_ref),
                (bl_in, bl_ref),
            ]
        )
    ]
    pl.semaphore_wait(barrier, len(peers))
    for load in loads[2:4]:
        load.wait()
    w1 = [links.push(wq.at[x, c, y], wq.at[x, c, y], dy=k) for k in Y_STEPS]
    for load in loads[:2]:
        load.wait()
    keys = Gather(links, kall)
    keys.first_a()
    keys.first_b()
    ev1 = []
    for to in Z_PEERS:
        there = pl.ds(pl.multiple_of(lax.rem(z + to["dz"], NZ) * 1024, 1024), 1024)
        ev1.append(links.push(ev_ref.at[0, :, there], evz.at[z], **to))
    for load in loads[4:]:
        load.wait()
    for e in range(8):
        ep8[e : e + 1, :] = ep_ref[:, e * BLOCK : (e + 1) * BLOCK]
    arrive(w1)
    w2 = [links.push(wq.at[x, c], wq.at[x, c], dx=k) for k in (2, 1, 3)]
    w3 = [links.push(wq.at[x, c], wq.at[x, c], dc=1)]
    arrive(keys.a1)
    keys.second_a()
    keys.second_b()
    for k, copy in zip((2, 1, 3), w2):
        copy.wait_recv()
        block = wq.at[lax.rem(x + NX - k, NX), c]
        w3.append(links.push(block, block, dc=1))
    arrive(ev1)
    arrive(w3)
    for a in range(NX):
        for b in range(2):
            for k in range(NY):
                low = (a * 2 + b) * 16
                wz[k, low : low + 16] = wq[a, b, k]
    partial = dot(evz[...].reshape(128, 1024), wz[...].reshape(1024, 256), 1, 0)
    pz0[...] = partial[:, :DH].reshape(NZ, 32, DH).astype(bf16)
    pz1[...] = partial[:, DH:].reshape(NZ, 32, DH).astype(bf16)
    z1a = [
        links.push(pz0.at[lax.rem(z + to["dz"], NZ)], rz0.at[to["dz"] - 1], **to) for to in Z_PEERS
    ]
    z1b = [
        links.push(pz1.at[lax.rem(z + to["dz"], NZ)], rz1.at[to["dz"] - 1], **to) for to in Z_PEERS
    ]
    patients = []
    for n in range(notes):
        row = np_ref[:, n * BLOCK : (n + 1) * BLOCK]
        patients.append(jnp.broadcast_to(row, (BLOCK, BLOCK)).T)

    def chosen(buf, e):
        return buf[e // 2, pl.ds((e % 2) * 4, 4)].reshape(BLOCK, DH)

    def spread_out(dst, h, n, first, second):
        ids = (bl_ref[0, 0, n], bl_ref[0, 1, n])
        none = jnp.zeros_like(first)
        for e in range(8):
            tile = jnp.where(ids[0] == e, first, jnp.where(ids[1] == e, second, none))
            dst[h, n * BLOCK : (n + 1) * BLOCK, e * BLOCK : (e + 1) * BLOCK] = tile

    def head(h):
        return slice(h * DH, (h + 1) * DH)

    handed = []

    def hand(src, dst):
        handed.append(links.fetch(src, dst, out_sem.at[len(handed)]))

    def share_head(h):
        low = (lz0, lz1)[h][...].reshape(128, DH)
        pw[h] = dot(evt[...], low, 1, 0).astype(bf16).reshape(NY, NX, 2, 16, DH)
        return links.push(pw.at[h, :, :, 1 - c], pr.at[h], dc=1)

    def sum_head(h, copy):
        copy.wait_recv()
        xs[h] = (pw[h, :, :, c].astype(f32) + pr[h].astype(f32)).astype(bf16)
        return [
            links.push(xs.at[h, :, lax.rem(x + k, NX)], xr.at[h, k - 1], dx=k) for k in (2, 1, 3)
        ]

    def score_head(h):
        for n in range(notes):
            q = q_ref[0, n * BLOCK : (n + 1) * BLOCK, head(h)]
            masked = []
            for slot in range(2):
                e = bl_ref[0, slot, n]
                s = dot(q, chosen(kall[h], e), 1, 1) * scale
                allow = patients[n] == ep8[pl.ds(e, 1), :]
                masked.append(jnp.where(allow, s, masked_score))
            top = jnp.max(jnp.maximum(masked[0], masked[1]), axis=1, keepdims=True)
            weight = [jnp.exp(s - top) for s in masked]
            row_sum = jnp.sum(weight[0] + weight[1], axis=1, keepdims=True)
            inverse = 1.0 / row_sum
            prob = [w * inverse for w in weight]
            for slot in range(2):
                probs[h, n, slot] = prob[slot]
            spread_out(pd, h, n, prob[0].astype(bf16), prob[1].astype(bf16))
        dvs[h] = dot(pd[h], g_ref[0, :, head(h)], 0, 0).astype(bf16).reshape(NZ, NY, 32, DH)

    def value_head(h):
        att = dot(pd[h], vall[h][...].reshape(1024, DH), 1, 0).astype(bf16)
        att_ref[0, :, head(h)] = att
        grad = g_ref[0, :, head(h)]
        delta = jnp.sum(grad.astype(f32) * att.astype(f32), axis=1, keepdims=True)
        for n in range(notes):
            rows = slice(n * BLOCK, (n + 1) * BLOCK)
            low = []
            for slot in range(2):
                pg = dot(grad[rows], chosen(vall[h], bl_ref[0, slot, n]), 1, 1)
                low.append((probs[h, n, slot] * (pg - delta[rows])).astype(bf16))
            spread_out(sd, h, n, low[0], low[1])
        dks[h] = dot(sd[h], q_ref[0, :, head(h)], 0, 0).astype(bf16).reshape(NZ, NY, 32, DH)

    def query_head(h):
        qg = dot(sd[h], kall[h][...].reshape(1024, DH), 1, 0) * scale
        qg_ref[0, :, head(h)] = qg.astype(bf16)
    value_sums = Scatter(links, dvs, va1, vb1, vsa, vsb, vfa, vfb, va2, vb2)
    key_sums = Scatter(links, dks, ka1, kb1, ksa, ksb, kfa, kfb, ka2, kb2)
    keys.done_a()
    score_head(0)
    value_sums.first_a()
    keys.done_b()
    score_head(1)
    value_sums.first_b()
    values = Gather(links, vall)
    arrive(z1a)
    own = pz0[z].astype(f32)
    for k in range(NZ - 1):
        own = own + rz0[k].astype(f32)
    v0[z, y] = own.astype(bf16)
    values.first_a()
    arrive(z1b)
    own = pz1[z].astype(f32)
    for k in range(NZ - 1):
        own = own + rz1[k].astype(f32)
    v1[z, y] = own.astype(bf16)
    values.first_b()
    evt[...] = evz[...].reshape(128, 1024).T
    value_sums.second_a(whole=True)
    value_sums.second_b()
    arrive(values.a1)
    values.second_a()
    values.second_b()
    lz1[z] = value_sums.done_b().astype(bf16)
    low1 = [links.push(lz1.at[z], lz1.at[z], **to) for to in Z_PEERS]
    lz0[...] = value_sums.done_a(whole=True).astype(bf16)
    c10 = share_head(0)
    x10 = sum_head(0, c10)
    values.done_a()
    value_head(0)
    key_sums.first_a()
    arrive(low1)
    c11 = share_head(1)
    x11 = sum_head(1, c11)
    values.done_b()
    value_head(1)
    key_sums.first_b()
    hand(att_ref, att_out)
    for h, copies in ((0, x10), (1, x11)):
        arrive(copies)
        total = xs[h, :, x].astype(f32)
        for k in range(NX - 1):
            total = total + xr[h, k].astype(f32)
        ys[:, :, head(h)] = total.astype(bf16)
    y1 = [links.push(ys.at[lax.rem(y + k, NY)], yr.at[k - 1], dy=k) for k in Y_STEPS]
    arrive(y1)
    total = ys[y].astype(f32)
    for k in range(NY - 1):
        total = total + yr[k].astype(f32)
    sh2[...] = total.astype(bf16)
    far = links.push(sh2, rzh, dzh=1)
    low_rows = jnp.concatenate([lz0[...].reshape(128, DH), lz1[...].reshape(128, DH)], axis=1)
    egs[...] = dot(low_rows, wz[...].reshape(1024, 256), 1, 1).astype(bf16).reshape(NZ, 32, 1024)
    e1 = [
        links.push(egs.at[lax.rem(z + to["dz"], NZ)], egr.at[z], **to) for to in Z_PEERS
    ]
    egr[z] = egs[z]
    for h in range(2):
        query_head(h)
    hand(qg_ref, qg_out)
    key_sums.second_a()
    far.wait_recv()
    sh3[...] = sh2[...].astype(f32) + rzh[...].astype(f32)
    x2 = [links.push(sh3, r2.at[part], **to) for to in XC_PEERS]
    r2[part] = sh3[...]
    key_sums.second_b()
    arrive(e1)
    for k in range(NZ):
        hand(egr.at[k], eg_out.at[0, :, k * 1024 : (k + 1) * 1024])
    kg_ref[0, :, head(0)] = (key_sums.done_a() * scale).astype(bf16)
    kg_ref[0, :, head(1)] = (key_sums.done_b() * scale).astype(bf16)
    hand(kg_ref, kg_out)
    arrive(x2)
    hand(r2, wg_out)
    for copy in handed:
        copy.wait()
    links.finish()


def scatter_scratch(whole):
    return [
        pltpu.VMEM((NY - 1, NZ, 32, DH), bf16),
        pltpu.VMEM((NZ - 1, NY, 32, DH), bf16),
        pltpu.VMEM((NZ, 32, DH), bf16),
        pltpu.VMEM((NY, 32, DH), bf16),
        pltpu.VMEM((NZ, 32, DH), f32),
        pltpu.VMEM((NY, 32, DH), f32),
        pltpu.VMEM((NZ - 1, NZ, 32, DH) if whole else (NZ - 1, 32, DH), bf16),
        pltpu.VMEM((NY - 1, 32, DH), bf16),
    ]


def hand_over(*refs):
    for i in range(5):
        refs[5 + i][...] = refs[i][...].reshape(refs[5 + i].shape)


def shards(*args):
    def shape(s, t):
        return jax.ShapeDtypeStruct(s, t)

    pair = pltpu.VMEM((2, NZ, NY, 32, DH), bf16)
    single = pltpu.VMEM((NZ, NY, 32, DH), bf16)
    results = pl.pallas_call(
        kernel,
        out_shape=(
            shape((1, 512, 256), bf16),
            shape((1, 512, 256), bf16),
            shape((1, 32, 256), bf16),
            shape((1, 32, 4096), bf16),
            shape((8, 16, 256), f32),
        ),
        in_specs=[pl.BlockSpec(memory_space=pl.ANY)] * 8,
        out_specs=(pl.BlockSpec(memory_space=pl.ANY),) * 5,
        scratch_shapes=[single] * 4
        + [pair] * 2
        + [
            pltpu.VMEM((NX, 2, NY, 16, 256), bf16),
            pltpu.VMEM((NY, 128, 256), bf16),
            pltpu.VMEM((NZ, 32, 1024), bf16),
            pltpu.VMEM((NZ, 32, DH), bf16),
            pltpu.VMEM((NZ, 32, DH), bf16),
            pltpu.VMEM((NZ - 1, 32, DH), bf16),
            pltpu.VMEM((NZ - 1, 32, DH), bf16),
            pltpu.VMEM((1024, 128), bf16),
            pltpu.VMEM((NZ, 32, 1024), bf16),
            pltpu.VMEM((NZ, 32, 1024), bf16),
            pltpu.VMEM((8, BLOCK), jnp.int32),
            pltpu.VMEM((2, 4, 2, BLOCK, BLOCK), f32),
            pltpu.VMEM((2, 512, 1024), bf16),
            pltpu.VMEM((2, 512, 1024), bf16),
            pltpu.VMEM((NZ, 32, DH), bf16),
            pltpu.VMEM((NZ, 32, DH), bf16),
            pltpu.VMEM((2, NY, NX, 2, 16, DH), bf16),
            pltpu.VMEM((2, NY, NX, 16, DH), bf16),
            pltpu.VMEM((2, NY, NX, 16, DH), bf16),
            pltpu.VMEM((2, NX - 1, NY, 16, DH), bf16),
            pltpu.VMEM((NY, 16, 256), bf16),
            pltpu.VMEM((NY - 1, 16, 256), bf16),
            pltpu.VMEM((16, 256), bf16),
            pltpu.VMEM((16, 256), bf16),
            pltpu.VMEM((16, 256), f32),
            pltpu.VMEM((8, 16, 256), f32),
        ]
        + scatter_scratch(True)
        + scatter_scratch(False)
        + [
            pltpu.VMEM((1, 512, 256), bf16),
            pltpu.VMEM((1, 32, 4096), bf16),
            pltpu.VMEM((1, 512, 256), bf16),
            pltpu.VMEM((1, 512), jnp.int32),
            pltpu.VMEM((1, 1024), jnp.int32),
            pltpu.SMEM((1, 2, 4), jnp.int32),
            pltpu.VMEM((1, 512, 256), bf16),
            pltpu.VMEM((1, 512, 256), bf16),
            pltpu.VMEM((1, 32, 256), bf16),
            pltpu.SemaphoreType.DMA((10,)),
            pltpu.SemaphoreType.DMA((8,)),
        ]
        + [pltpu.SemaphoreType.DMA((160,)), pltpu.SemaphoreType.DMA((160,))],
        compiler_params=pltpu.CompilerParams(
            collective_id=0, has_side_effects=True, vmem_limit_bytes=60 * 1024 * 1024
        ),
        name="notes",
    )(*args[:7], jnp.swapaxes(args[7], 1, 2))
    return pl.pallas_call(
        hand_over,
        out_shape=tuple(shape(r.shape, r.dtype) for r in results[:4]) + (shape((128, 256), f32),),
        name="hand_over",
    )(*results)


def solution(mesh):
    return jax.shard_map(
        shards,
        mesh=mesh,
        in_specs=(
            P("dp", "blk", None),
            P("dp", "blk", None),
            P("dp", "blk", None),
            P("blk", None),
            P("dp", "blk", None),
            P("dp", "blk"),
            P("dp", None),
            P("dp", "blk", None),
        ),
        out_specs=(
            P("dp", "blk", None),
            P("dp", "blk", None),
            P("dp", "blk", None),
            P("dp", "blk", None),
            P("blk", None),
        ),
        check_vma=False,
    )
```

```python
import functools
import math

import jax
import jax.numpy as jnp
from jax import lax
from jax.experimental import pallas as pl
from jax.experimental.pallas import tpu as pltpu
from jax.sharding import PartitionSpec as P

MESH = pl.DeviceIdType.MESH
DH = 128
BLOCK = 128
NZ, NY, NX = 4, 8, 4
masked_score = -1e30
scale = 1.0 / math.sqrt(DH)
f32 = jnp.float32
bf16 = jnp.bfloat16

Z_PEERS = [dict(dz=k) for k in (1, 3, 2)]
Y_STEPS = (4, 3, 5, 2, 6, 1, 7)
XC_PEERS = [dict(dx=a, dc=b) for a in (2, 1, 3, 0) for b in (0, 1) if (a, b) != (0, 0)]
ZH_PEERS = [dict(dzh=1)]


def place():
    blk = lax.axis_index("blk")
    dp = lax.axis_index("dp")
    return blk // NY, blk % NY, dp // 8, (dp // 2) % NX, dp % 2


def device(dz=0, dy=0, dzh=0, dx=0, dc=0):
    z, y, zh, x, c = place()
    return {
        "blk": lax.rem(z + dz, NZ) * NY + lax.rem(y + dy, NY),
        "dp": lax.rem(zh + dzh, 2) * 8 + lax.rem(x + dx, NX) * 2 + lax.rem(c + dc, 2),
    }


class Links:
    def __init__(self, send_sem, recv_sem):
        self.send_sem, self.recv_sem, self.count, self.started = send_sem, recv_sem, 0, []

    def push(self, src, dst, **to):
        index = self.count
        self.count += 1
        copy = pltpu.make_async_remote_copy(
            src_ref=src,
            dst_ref=dst,
            send_sem=self.send_sem.at[index],
            recv_sem=self.recv_sem.at[index],
            device_id=device(**to),
            device_id_type=MESH,
        )
        copy.start()
        self.started.append(copy)
        return copy

    def burst(self, whole, pushes):
        index = self.count
        self.count += 1

        def copy(src, dst, to):
            return pltpu.make_async_remote_copy(
                src_ref=src,
                dst_ref=dst,
                send_sem=self.send_sem.at[index],
                recv_sem=self.recv_sem.at[index],
                device_id=device(**to),
                device_id_type=MESH,
            )

        for src, dst, to in pushes:
            copy(src, dst, to).start()
        total = copy(whole, whole, dict(dc=1))
        self.started.append(total)
        return [total]

    def fetch(self, src, dst, sem):
        copy = pltpu.make_async_copy(src, dst, sem)
        copy.start()
        return copy

    def finish(self):
        for copy in self.started:
            copy.wait_send()


def arrive(copies):
    for copy in copies:
        copy.wait_recv()


def dot(a, b, ca, cb):
    return lax.dot_general(a, b, (((ca,), (cb,)), ((), ())), preferred_element_type=f32)


class Gather:
    def __init__(self, links, buf):
        self.links, self.buf = links, buf
        self.z, self.y = place()[:2]

    def first_a(self):
        z, y, buf = self.z, self.y, self.buf
        self.a1 = self.links.burst(
            buf[0].at[0, pl.ds(0, 3)], [(buf[0].at[z, y], buf[0].at[z, y], to) for to in Z_PEERS]
        )

    def first_b(self):
        z, y, buf = self.z, self.y, self.buf
        self.b1 = self.links.burst(
            buf[1].at[0, pl.ds(0, 7)],
            [(buf[1].at[z, y], buf[1].at[z, y], dict(dy=k)) for k in Y_STEPS],
        )

    def second_a(self):
        y, buf = self.y, self.buf
        self.a2 = self.links.burst(
            buf[0].at[:, pl.ds(0, 7)],
            [(buf[0].at[:, y], buf[0].at[:, y], dict(dy=k)) for k in Y_STEPS],
        )

    def second_b(self):
        arrive(self.b1)
        z, buf = self.z, self.buf
        self.b2 = self.links.burst(
            buf[1].at[pl.ds(0, 3)], [(buf[1].at[z], buf[1].at[z], to) for to in Z_PEERS]
        )

    def done_a(self):
        arrive(self.a2)

    def done_b(self):
        arrive(self.b2)


class Scatter:
    def __init__(self, links, src, ra1, rb1, sa, sb, fa, fb, ra2, rb2):
        self.links, self.src, self.ra1, self.rb1 = links, src, ra1, rb1
        self.sa, self.sb, self.fa, self.fb, self.ra2, self.rb2 = sa, sb, fa, fb, ra2, rb2
        self.z, self.y = place()[:2]

    def first_a(self):
        self.a1 = self.links.burst(
            self.ra1,
            [
                (self.src.at[0, :, lax.rem(self.y + k, NY)], self.ra1.at[k - 1], dict(dy=k))
                for k in Y_STEPS
            ],
        )

    def first_b(self):
        self.b1 = self.links.burst(
            self.rb1,
            [
                (self.src.at[1, lax.rem(self.z + to["dz"], NZ)], self.rb1.at[to["dz"] - 1], to)
                for to in Z_PEERS
            ],
        )

    def second_a(self, whole=False):
        arrive(self.a1)
        total = self.src[0, :, self.y].astype(f32)
        for k in range(NY - 1):
            total = total + self.ra1[k].astype(f32)
        self.fa[...] = total
        self.sa[...] = total.astype(bf16)
        self.a2 = self.links.burst(
            self.ra2,
            [
                (
                    self.sa if whole else self.sa.at[lax.rem(self.z + to["dz"], NZ)],
                    self.ra2.at[to["dz"] - 1],
                    to,
                )
                for to in Z_PEERS
            ],
        )

    def second_b(self):
        arrive(self.b1)
        total = self.src[1, self.z].astype(f32)
        for k in range(NZ - 1):
            total = total + self.rb1[k].astype(f32)
        self.fb[...] = total
        self.sb[...] = total.astype(bf16)
        self.b2 = self.links.burst(
            self.rb2,
            [
                (self.sb.at[lax.rem(self.y + k, NY)], self.rb2.at[k - 1], dict(dy=k))
                for k in Y_STEPS
            ],
        )

    def done_a(self, whole=False):
        arrive(self.a2)
        total = self.fa[...] if whole else self.fa[self.z]
        for k in range(NZ - 1):
            total = total + self.ra2[k].astype(f32)
        return total

    def done_b(self):
        arrive(self.b2)
        total = self.fb[self.y]
        for k in range(NY - 1):
            total = total + self.rb2[k].astype(f32)
        return total


def kernel(
    q_in, k_in, ev_in, w_in, g_in, np_in, ep_in, bl_in,
    att_out, qg_out, kg_out, eg_out, wg_out,
    k0, k1, v0, v1, dvs, dks, wq, wz, evz, pz0, pz1, rz0, rz1, evt, egs, egr,
    ep8, probs, pd, sd, lz0, lz1, pw, pr, xs, xr, ys, yr, sh2, rzh, sh3, r2,
    va1, vb1, vsa, vsb, vfa, vfb, va2, vb2,
    ka1, kb1, ksa, ksb, kfa, kfb, ka2, kb2,
    q_ref, ev_ref, g_ref, np_ref, ep_ref, bl_ref, att_ref, qg_ref, kg_ref, in_sem, out_sem, send_sem, recv_sem,
):
    kall, vall = (k0, k1), (v0, v1)
    z, y, zh, x, c = place()
    part = x * 2 + c
    notes = q_ref.shape[1] // BLOCK
    barrier = pltpu.get_barrier_semaphore()
    peers = ZH_PEERS + [dict(dy=k) for k in Y_STEPS] + Z_PEERS + XC_PEERS
    for to in peers:
        pl.semaphore_signal(barrier, inc=1, device_id=device(**to), device_id_type=MESH)
    links = Links(send_sem, recv_sem)
    own_cols = pl.ds(pl.multiple_of(z * 1024, 1024), 1024)
    loads = [
        links.fetch(src, dst, in_sem.at[i])
        for i, (src, dst) in enumerate(
            [
                (k_in.at[0, :, :DH], k0.at[z, y]),
                (k_in.at[0, :, DH:], k1.at[z, y]),
                (w_in.at[pl.ds(pl.multiple_of(part * 16, 16), 16)], wq.at[x, c, y]),
                (ev_in, ev_ref),
                (ev_in.at[0, :, own_cols], evz.at[z]),
                (q_in, q_ref),
                (g_in, g_ref),
                (np_in, np_ref),
                (ep_in, ep_ref),
                (bl_in, bl_ref),
            ]
        )
    ]
    pl.semaphore_wait(barrier, len(peers))
    for load in loads[2:4]:
        load.wait()
    w1 = links.burst(
        wq.at[0, 0, pl.ds(0, 7)],
        [(wq.at[x, c, y], wq.at[x, c, y], dict(dy=k)) for k in Y_STEPS],
    )
    for load in loads[:2]:
        load.wait()
    keys = Gather(links, kall)
    keys.first_a()
    keys.first_b()
    ev1 = []
    for to in Z_PEERS:
        there = pl.ds(pl.multiple_of(lax.rem(z + to["dz"], NZ) * 1024, 1024), 1024)
        ev1.append((ev_ref.at[0, :, there], evz.at[z], to))
    ev1 = links.burst(evz.at[pl.ds(0, 3)], ev1)
    for load in loads[4:]:
        load.wait()
    for e in range(8):
        ep8[e : e + 1, :] = ep_ref[:, e * BLOCK : (e + 1) * BLOCK]
    arrive(w1)
    w2 = [links.push(wq.at[x, c], wq.at[x, c], dx=k) for k in (2, 1, 3)]
    w3 = [links.push(wq.at[x, c], wq.at[x, c], dc=1)]
    arrive(keys.a1)
    keys.second_a()
    keys.second_b()
    for k, copy in zip((2, 1, 3), w2):
        copy.wait_recv()
        block = wq.at[lax.rem(x + NX - k, NX), c]
        w3.append(links.push(block, block, dc=1))
    arrive(ev1)
    arrive(w3)
    for a in range(NX):
        for b in range(2):
            for k in range(NY):
                low = (a * 2 + b) * 16
                wz[k, low : low + 16] = wq[a, b, k]
    partial = dot(evz[...].reshape(128, 1024), wz[...].reshape(1024, 256), 1, 0)
    pz0[...] = partial[:, :DH].reshape(NZ, 32, DH).astype(bf16)
    pz1[...] = partial[:, DH:].reshape(NZ, 32, DH).astype(bf16)
    z1a = links.burst(
        rz0,
        [
            (pz0.at[lax.rem(z + to["dz"], NZ)], rz0.at[to["dz"] - 1], to)
            for to in Z_PEERS
        ],
    )
    z1b = links.burst(
        rz1,
        [
            (pz1.at[lax.rem(z + to["dz"], NZ)], rz1.at[to["dz"] - 1], to)
            for to in Z_PEERS
        ],
    )
    patients = []
    for n in range(notes):
        row = np_ref[:, n * BLOCK : (n + 1) * BLOCK]
        patients.append(jnp.broadcast_to(row, (BLOCK, BLOCK)).T)

    def chosen(buf, e):
        return buf[e // 2, pl.ds((e % 2) * 4, 4)].reshape(BLOCK, DH)

    def spread_out(dst, h, n, first, second):
        ids = (bl_ref[0, 0, n], bl_ref[0, 1, n])
        none = jnp.zeros_like(first)
        for e in range(8):
            tile = jnp.where(ids[0] == e, first, jnp.where(ids[1] == e, second, none))
            dst[h, n * BLOCK : (n + 1) * BLOCK, e * BLOCK : (e + 1) * BLOCK] = tile

    def head(h):
        return slice(h * DH, (h + 1) * DH)

    handed = []

    def hand(src, dst):
        handed.append(links.fetch(src, dst, out_sem.at[len(handed)]))

    def share_head(h):
        low = (lz0, lz1)[h][...].reshape(128, DH)
        pw[h] = dot(evt[...], low, 1, 0).astype(bf16).reshape(NY, NX, 2, 16, DH)
        return links.push(pw.at[h, :, :, 1 - c], pr.at[h], dc=1)

    def sum_head(h, copy):
        copy.wait_recv()
        xs[h] = (pw[h, :, :, c].astype(f32) + pr[h].astype(f32)).astype(bf16)
        return links.burst(
            xr.at[h],
            [
                (xs.at[h, :, lax.rem(x + k, NX)], xr.at[h, k - 1], dict(dx=k))
                for k in (2, 1, 3)
            ],
        )

    def score_head(h):
        for n in range(notes):
            q = q_ref[0, n * BLOCK : (n + 1) * BLOCK, head(h)]
            masked = []
            for slot in range(2):
                e = bl_ref[0, slot, n]
                s = dot(q, chosen(kall[h], e), 1, 1) * scale
                allow = patients[n] == ep8[pl.ds(e, 1), :]
                masked.append(jnp.where(allow, s, masked_score))
            top = jnp.max(jnp.maximum(masked[0], masked[1]), axis=1, keepdims=True)
            weight = [jnp.exp(s - top) for s in masked]
            row_sum = jnp.sum(weight[0] + weight[1], axis=1, keepdims=True)
            inverse = 1.0 / row_sum
            prob = [w * inverse for w in weight]
            for slot in range(2):
                probs[h, n, slot] = prob[slot]
            spread_out(pd, h, n, prob[0].astype(bf16), prob[1].astype(bf16))
        dvs[h] = dot(pd[h], g_ref[0, :, head(h)], 0, 0).astype(bf16).reshape(NZ, NY, 32, DH)

    def value_head(h):
        att = dot(pd[h], vall[h][...].reshape(1024, DH), 1, 0).astype(bf16)
        att_ref[0, :, head(h)] = att
        grad = g_ref[0, :, head(h)]
        delta = jnp.sum(grad.astype(f32) * att.astype(f32), axis=1, keepdims=True)
        for n in range(notes):
            rows = slice(n * BLOCK, (n + 1) * BLOCK)
            low = []
            for slot in range(2):
                pg = dot(grad[rows], chosen(vall[h], bl_ref[0, slot, n]), 1, 1)
                low.append((probs[h, n, slot] * (pg - delta[rows])).astype(bf16))
            spread_out(sd, h, n, low[0], low[1])
        dks[h] = dot(sd[h], q_ref[0, :, head(h)], 0, 0).astype(bf16).reshape(NZ, NY, 32, DH)

    def query_head(h):
        qg = dot(sd[h], kall[h][...].reshape(1024, DH), 1, 0) * scale
        qg_ref[0, :, head(h)] = qg.astype(bf16)
    value_sums = Scatter(links, dvs, va1, vb1, vsa, vsb, vfa, vfb, va2, vb2)
    key_sums = Scatter(links, dks, ka1, kb1, ksa, ksb, kfa, kfb, ka2, kb2)
    keys.done_a()
    score_head(0)
    value_sums.first_a()
    keys.done_b()
    score_head(1)
    value_sums.first_b()
    values = Gather(links, vall)
    arrive(z1a)
    own = pz0[z].astype(f32)
    for k in range(NZ - 1):
        own = own + rz0[k].astype(f32)
    v0[z, y] = own.astype(bf16)
    values.first_a()
    arrive(z1b)
    own = pz1[z].astype(f32)
    for k in range(NZ - 1):
        own = own + rz1[k].astype(f32)
    v1[z, y] = own.astype(bf16)
    values.first_b()
    evt[...] = evz[...].reshape(128, 1024).T
    value_sums.second_a(whole=True)
    value_sums.second_b()
    arrive(values.a1)
    values.second_a()
    values.second_b()
    lz1[z] = value_sums.done_b().astype(bf16)
    low1 = links.burst(lz1.at[pl.ds(0, 3)], [(lz1.at[z], lz1.at[z], to) for to in Z_PEERS])
    lz0[...] = value_sums.done_a(whole=True).astype(bf16)
    c10 = share_head(0)
    x10 = sum_head(0, c10)
    values.done_a()
    value_head(0)
    key_sums.first_a()
    arrive(low1)
    c11 = share_head(1)
    x11 = sum_head(1, c11)
    values.done_b()
    value_head(1)
    key_sums.first_b()
    hand(att_ref, att_out)
    for h, copies in ((0, x10), (1, x11)):
        arrive(copies)
        total = xs[h, :, x].astype(f32)
        for k in range(NX - 1):
            total = total + xr[h, k].astype(f32)
        ys[:, :, head(h)] = total.astype(bf16)
    y1 = links.burst(
        yr, [(ys.at[lax.rem(y + k, NY)], yr.at[k - 1], dict(dy=k)) for k in Y_STEPS]
    )
    for h in range(2):
        query_head(h)
    hand(qg_ref, qg_out)
    arrive(y1)
    total = ys[y].astype(f32)
    for k in range(NY - 1):
        total = total + yr[k].astype(f32)
    sh2[...] = total.astype(bf16)
    far = links.push(sh2, rzh, dzh=1)
    low_rows = jnp.concatenate([lz0[...].reshape(128, DH), lz1[...].reshape(128, DH)], axis=1)
    egs[...] = dot(low_rows, wz[...].reshape(1024, 256), 1, 1).astype(bf16).reshape(NZ, 32, 1024)
    e1 = links.burst(
        egr.at[pl.ds(0, 3)],
        [(egs.at[lax.rem(z + to["dz"], NZ)], egr.at[z], to) for to in Z_PEERS],
    )
    egr[z] = egs[z]
    key_sums.second_a()
    far.wait_recv()
    sh3[...] = sh2[...].astype(f32) + rzh[...].astype(f32)
    x2 = links.burst(r2.at[pl.ds(0, 7)], [(sh3, r2.at[part], to) for to in XC_PEERS])
    r2[part] = sh3[...]
    key_sums.second_b()
    arrive(e1)
    for k in range(NZ):
        hand(egr.at[k], eg_out.at[0, :, k * 1024 : (k + 1) * 1024])
    kg_ref[0, :, head(0)] = (key_sums.done_a() * scale).astype(bf16)
    kg_ref[0, :, head(1)] = (key_sums.done_b() * scale).astype(bf16)
    hand(kg_ref, kg_out)
    arrive(x2)
    hand(r2, wg_out)
    for copy in handed:
        copy.wait()
    links.finish()


def scatter_scratch(whole):
    return [
        pltpu.VMEM((NY - 1, NZ, 32, DH), bf16),
        pltpu.VMEM((NZ - 1, NY, 32, DH), bf16),
        pltpu.VMEM((NZ, 32, DH), bf16),
        pltpu.VMEM((NY, 32, DH), bf16),
        pltpu.VMEM((NZ, 32, DH), f32),
        pltpu.VMEM((NY, 32, DH), f32),
        pltpu.VMEM((NZ - 1, NZ, 32, DH) if whole else (NZ - 1, 32, DH), bf16),
        pltpu.VMEM((NY - 1, 32, DH), bf16),
    ]


def hand_over(*refs):
    for i in range(5):
        refs[5 + i][...] = refs[i][...].reshape(refs[5 + i].shape)


def shards(*args):
    def shape(s, t):
        return jax.ShapeDtypeStruct(s, t)

    pair = pltpu.VMEM((2, NZ, NY, 32, DH), bf16)
    single = pltpu.VMEM((NZ, NY, 32, DH), bf16)
    results = pl.pallas_call(
        kernel,
        out_shape=(
            shape((1, 512, 256), bf16),
            shape((1, 512, 256), bf16),
            shape((1, 32, 256), bf16),
            shape((1, 32, 4096), bf16),
            shape((8, 16, 256), f32),
        ),
        in_specs=[pl.BlockSpec(memory_space=pl.ANY)] * 8,
        out_specs=(pl.BlockSpec(memory_space=pl.ANY),) * 5,
        scratch_shapes=[single] * 4
        + [pair] * 2
        + [
            pltpu.VMEM((NX, 2, NY, 16, 256), bf16),
            pltpu.VMEM((NY, 128, 256), bf16),
            pltpu.VMEM((NZ, 32, 1024), bf16),
            pltpu.VMEM((NZ, 32, DH), bf16),
            pltpu.VMEM((NZ, 32, DH), bf16),
            pltpu.VMEM((NZ - 1, 32, DH), bf16),
            pltpu.VMEM((NZ - 1, 32, DH), bf16),
            pltpu.VMEM((1024, 128), bf16),
            pltpu.VMEM((NZ, 32, 1024), bf16),
            pltpu.VMEM((NZ, 32, 1024), bf16),
            pltpu.VMEM((8, BLOCK), jnp.int32),
            pltpu.VMEM((2, 4, 2, BLOCK, BLOCK), f32),
            pltpu.VMEM((2, 512, 1024), bf16),
            pltpu.VMEM((2, 512, 1024), bf16),
            pltpu.VMEM((NZ, 32, DH), bf16),
            pltpu.VMEM((NZ, 32, DH), bf16),
            pltpu.VMEM((2, NY, NX, 2, 16, DH), bf16),
            pltpu.VMEM((2, NY, NX, 16, DH), bf16),
            pltpu.VMEM((2, NY, NX, 16, DH), bf16),
            pltpu.VMEM((2, NX - 1, NY, 16, DH), bf16),
            pltpu.VMEM((NY, 16, 256), bf16),
            pltpu.VMEM((NY - 1, 16, 256), bf16),
            pltpu.VMEM((16, 256), bf16),
            pltpu.VMEM((16, 256), bf16),
            pltpu.VMEM((16, 256), f32),
            pltpu.VMEM((8, 16, 256), f32),
        ]
        + scatter_scratch(True)
        + scatter_scratch(False)
        + [
            pltpu.VMEM((1, 512, 256), bf16),
            pltpu.VMEM((1, 32, 4096), bf16),
            pltpu.VMEM((1, 512, 256), bf16),
            pltpu.VMEM((1, 512), jnp.int32),
            pltpu.VMEM((1, 1024), jnp.int32),
            pltpu.SMEM((1, 2, 4), jnp.int32),
            pltpu.VMEM((1, 512, 256), bf16),
            pltpu.VMEM((1, 512, 256), bf16),
            pltpu.VMEM((1, 32, 256), bf16),
            pltpu.SemaphoreType.DMA((10,)),
            pltpu.SemaphoreType.DMA((8,)),
        ]
        + [pltpu.SemaphoreType.DMA((36,)), pltpu.SemaphoreType.DMA((36,))],
        compiler_params=pltpu.CompilerParams(
            collective_id=0, has_side_effects=True, vmem_limit_bytes=60 * 1024 * 1024
        ),
        name="notes",
    )(*args[:7], jnp.swapaxes(args[7], 1, 2))
    return pl.pallas_call(
        hand_over,
        out_shape=tuple(shape(r.shape, r.dtype) for r in results[:4]) + (shape((128, 256), f32),),
        name="hand_over",
    )(*results)


def solution(mesh):
    return jax.shard_map(
        shards,
        mesh=mesh,
        in_specs=(
            P("dp", "blk", None),
            P("dp", "blk", None),
            P("dp", "blk", None),
            P("blk", None),
            P("dp", "blk", None),
            P("dp", "blk"),
            P("dp", None),
            P("dp", "blk", None),
        ),
        out_specs=(
            P("dp", "blk", None),
            P("dp", "blk", None),
            P("dp", "blk", None),
            P("dp", "blk", None),
            P("blk", None),
        ),
        check_vma=False,
    )
```

```python
import functools
import math

import jax
import jax.numpy as jnp
from jax import lax
from jax.experimental import pallas as pl
from jax.experimental.pallas import tpu as pltpu
from jax.sharding import PartitionSpec as P

MESH = pl.DeviceIdType.MESH
DH = 128
BLOCK = 128
NZ, NY, NX = 4, 8, 4
masked_score = -1e30
scale = 1.0 / math.sqrt(DH)
f32 = jnp.float32
bf16 = jnp.bfloat16

Z_PEERS = [dict(dz=k) for k in (1, 3, 2)]
Y_STEPS = (4, 3, 5, 2, 6, 1, 7)
XC_PEERS = [dict(dx=a, dc=b) for a in (2, 1, 3, 0) for b in (0, 1) if (a, b) != (0, 0)]
ZH_PEERS = [dict(dzh=1)]


def place():
    blk = lax.axis_index("blk")
    dp = lax.axis_index("dp")
    return blk // NY, blk % NY, dp // 8, (dp // 2) % NX, dp % 2


def device(dz=0, dy=0, dzh=0, dx=0, dc=0):
    z, y, zh, x, c = place()
    return {
        "blk": lax.rem(z + dz, NZ) * NY + lax.rem(y + dy, NY),
        "dp": lax.rem(zh + dzh, 2) * 8 + lax.rem(x + dx, NX) * 2 + lax.rem(c + dc, 2),
    }


class Links:
    def __init__(self, send_sem, recv_sem):
        self.send_sem, self.recv_sem, self.count, self.started = send_sem, recv_sem, 0, []

    def push(self, src, dst, **to):
        index = self.count
        self.count += 1
        copy = pltpu.make_async_remote_copy(
            src_ref=src,
            dst_ref=dst,
            send_sem=self.send_sem.at[index],
            recv_sem=self.recv_sem.at[index],
            device_id=device(**to),
            device_id_type=MESH,
        )
        copy.start()
        self.started.append(copy)
        return copy

    def burst(self, whole, pushes):
        index = self.count
        self.count += 1

        def copy(src, dst, to):
            return pltpu.make_async_remote_copy(
                src_ref=src,
                dst_ref=dst,
                send_sem=self.send_sem.at[index],
                recv_sem=self.recv_sem.at[index],
                device_id=device(**to),
                device_id_type=MESH,
            )

        for src, dst, to in pushes:
            copy(src, dst, to).start()
        total = copy(whole, whole, dict(dc=1))
        self.started.append(total)
        return [total]

    def fetch(self, src, dst, sem):
        copy = pltpu.make_async_copy(src, dst, sem)
        copy.start()
        return copy

    def finish(self):
        for copy in self.started:
            copy.wait_send()


def arrive(copies):
    for copy in copies:
        copy.wait_recv()


def dot(a, b, ca, cb):
    return lax.dot_general(a, b, (((ca,), (cb,)), ((), ())), preferred_element_type=f32)


class Gather:
    def __init__(self, links, buf):
        self.links, self.buf = links, buf
        self.z, self.y = place()[:2]

    def first_a(self):
        z, y, buf = self.z, self.y, self.buf
        self.a1 = self.links.burst(
            buf[0].at[0, pl.ds(0, 3)], [(buf[0].at[z, y], buf[0].at[z, y], to) for to in Z_PEERS]
        )

    def first_b(self):
        z, y, buf = self.z, self.y, self.buf
        self.b1 = self.links.burst(
            buf[1].at[0, pl.ds(0, 7)],
            [(buf[1].at[z, y], buf[1].at[z, y], dict(dy=k)) for k in Y_STEPS],
        )

    def second_a(self):
        y, buf = self.y, self.buf
        self.a2 = self.links.burst(
            buf[0].at[:, pl.ds(0, 7)],
            [(buf[0].at[:, y], buf[0].at[:, y], dict(dy=k)) for k in Y_STEPS],
        )

    def second_b(self):
        arrive(self.b1)
        z, buf = self.z, self.buf
        self.b2 = self.links.burst(
            buf[1].at[pl.ds(0, 3)], [(buf[1].at[z], buf[1].at[z], to) for to in Z_PEERS]
        )

    def done_a(self):
        arrive(self.a2)

    def done_b(self):
        arrive(self.b2)


class Scatter:
    def __init__(self, links, src, ra1, rb1, sa, sb, fa, fb, ra2, rb2):
        self.links, self.src, self.ra1, self.rb1 = links, src, ra1, rb1
        self.sa, self.sb, self.fa, self.fb, self.ra2, self.rb2 = sa, sb, fa, fb, ra2, rb2
        self.z, self.y = place()[:2]

    def first_a(self):
        self.a1 = self.links.burst(
            self.ra1,
            [
                (self.src.at[0, :, lax.rem(self.y + k, NY)], self.ra1.at[k - 1], dict(dy=k))
                for k in Y_STEPS
            ],
        )

    def first_b(self):
        self.b1 = self.links.burst(
            self.rb1,
            [
                (self.src.at[1, lax.rem(self.z + to["dz"], NZ)], self.rb1.at[to["dz"] - 1], to)
                for to in Z_PEERS
            ],
        )

    def second_a(self, whole=False):
        arrive(self.a1)
        total = self.src[0, :, self.y].astype(f32)
        for k in range(NY - 1):
            total = total + self.ra1[k].astype(f32)
        self.fa[...] = total
        self.sa[...] = total.astype(bf16)
        self.a2 = self.links.burst(
            self.ra2,
            [
                (
                    self.sa if whole else self.sa.at[lax.rem(self.z + to["dz"], NZ)],
                    self.ra2.at[to["dz"] - 1],
                    to,
                )
                for to in Z_PEERS
            ],
        )

    def second_b(self):
        arrive(self.b1)
        total = self.src[1, self.z].astype(f32)
        for k in range(NZ - 1):
            total = total + self.rb1[k].astype(f32)
        self.fb[...] = total
        self.sb[...] = total.astype(bf16)
        self.b2 = self.links.burst(
            self.rb2,
            [
                (self.sb.at[lax.rem(self.y + k, NY)], self.rb2.at[k - 1], dict(dy=k))
                for k in Y_STEPS
            ],
        )

    def done_a(self, whole=False):
        arrive(self.a2)
        total = self.fa[...] if whole else self.fa[self.z]
        for k in range(NZ - 1):
            total = total + self.ra2[k].astype(f32)
        return total

    def done_b(self):
        arrive(self.b2)
        total = self.fb[self.y]
        for k in range(NY - 1):
            total = total + self.rb2[k].astype(f32)
        return total


def kernel(
    q_in, k_in, ev_in, w_in, g_in, np_in, ep_in, bl_in,
    att_out, qg_out, kg_out, eg_out, wg_out,
    k0, k1, v0, v1, dvs, dks, wq, wz, evz, pz0, pz1, rz0, rz1, evt, egs, egr,
    ep8, probs, pd, sd, lz0, lz1, pw, pr, xs, xr, ys, yr, sh2, rzh, sh3, r2,
    va1, vb1, vsa, vsb, vfa, vfb, va2, vb2,
    ka1, kb1, ksa, ksb, kfa, kfb, ka2, kb2,
    q_ref, ev_ref, g_ref, np_ref, ep_ref, bl_ref, att_ref, qg_ref, kg_ref, in_sem, out_sem, send_sem, recv_sem,
):
    kall, vall = (k0, k1), (v0, v1)
    z, y, zh, x, c = place()
    part = x * 2 + c
    notes = q_ref.shape[1] // BLOCK
    barrier = pltpu.get_barrier_semaphore()
    peers = ZH_PEERS + [dict(dy=k) for k in Y_STEPS] + Z_PEERS + XC_PEERS
    for to in peers:
        pl.semaphore_signal(barrier, inc=1, device_id=device(**to), device_id_type=MESH)
    links = Links(send_sem, recv_sem)
    own_cols = pl.ds(pl.multiple_of(z * 1024, 1024), 1024)
    loads = [
        links.fetch(src, dst, in_sem.at[i])
        for i, (src, dst) in enumerate(
            [
                (k_in.at[0, :, :DH], k0.at[z, y]),
                (k_in.at[0, :, DH:], k1.at[z, y]),
                (w_in.at[pl.ds(pl.multiple_of(part * 16, 16), 16)], wq.at[x, c, y]),
                (ev_in, ev_ref),
                (ev_in.at[0, :, own_cols], evz.at[z]),
                (q_in, q_ref),
                (g_in, g_ref),
                (np_in, np_ref),
                (ep_in, ep_ref),
                (bl_in, bl_ref),
            ]
        )
    ]
    pl.semaphore_wait(barrier, len(peers))
    for load in loads[2:4]:
        load.wait()
    w1 = links.burst(
        wq.at[0, 0, pl.ds(0, 7)],
        [(wq.at[x, c, y], wq.at[x, c, y], dict(dy=k)) for k in Y_STEPS],
    )
    for load in loads[:2]:
        load.wait()
    keys = Gather(links, kall)
    keys.first_a()
    keys.first_b()
    ev1 = []
    for to in Z_PEERS:
        there = pl.ds(pl.multiple_of(lax.rem(z + to["dz"], NZ) * 1024, 1024), 1024)
        ev1.append((ev_ref.at[0, :, there], evz.at[z], to))
    ev1 = links.burst(evz.at[pl.ds(0, 3)], ev1)
    for load in loads[4:]:
        load.wait()
    for e in range(8):
        ep8[e : e + 1, :] = ep_ref[:, e * BLOCK : (e + 1) * BLOCK]
    arrive(w1)
    w2 = [links.push(wq.at[x, c], wq.at[x, c], dx=k) for k in (2, 1, 3)]
    w3 = [links.push(wq.at[x, c], wq.at[x, c], dc=1)]
    arrive(keys.a1)
    keys.second_a()
    keys.second_b()
    for k, copy in zip((2, 1, 3), w2):
        copy.wait_recv()
        block = wq.at[lax.rem(x + NX - k, NX), c]
        w3.append(links.push(block, block, dc=1))
    arrive(ev1)
    arrive(w3)
    for a in range(NX):
        for b in range(2):
            for k in range(NY):
                low = (a * 2 + b) * 16
                wz[k, low : low + 16] = wq[a, b, k]
    partial = dot(evz[...].reshape(128, 1024), wz[...].reshape(1024, 256), 1, 0)
    pz0[...] = partial[:, :DH].reshape(NZ, 32, DH).astype(bf16)
    pz1[...] = partial[:, DH:].reshape(NZ, 32, DH).astype(bf16)
    z1a = links.burst(
        rz0,
        [
            (pz0.at[lax.rem(z + to["dz"], NZ)], rz0.at[to["dz"] - 1], to)
            for to in Z_PEERS
        ],
    )
    z1b = links.burst(
        rz1,
        [
            (pz1.at[lax.rem(z + to["dz"], NZ)], rz1.at[to["dz"] - 1], to)
            for to in Z_PEERS
        ],
    )
    patients = []
    for n in range(notes):
        row = np_ref[:, n * BLOCK : (n + 1) * BLOCK]
        patients.append(jnp.broadcast_to(row, (BLOCK, BLOCK)).T)

    def chosen(buf, e):
        return buf[e // 2, pl.ds((e % 2) * 4, 4)].reshape(BLOCK, DH)

    def spread_out(dst, h, n, first, second):
        ids = (bl_ref[0, 0, n], bl_ref[0, 1, n])
        none = jnp.zeros_like(first)
        for e in range(8):
            tile = jnp.where(ids[0] == e, first, jnp.where(ids[1] == e, second, none))
            dst[h, n * BLOCK : (n + 1) * BLOCK, e * BLOCK : (e + 1) * BLOCK] = tile

    def head(h):
        return slice(h * DH, (h + 1) * DH)

    handed = []

    def hand(src, dst):
        handed.append(links.fetch(src, dst, out_sem.at[len(handed)]))

    def share_head(h):
        low = (lz0, lz1)[h][...].reshape(128, DH)
        pw[h] = dot(evt[...], low, 1, 0).astype(bf16).reshape(NY, NX, 2, 16, DH)
        return links.push(pw.at[h, :, :, 1 - c], pr.at[h], dc=1)

    def sum_head(h, copy):
        copy.wait_recv()
        xs[h] = (pw[h, :, :, c].astype(f32) + pr[h].astype(f32)).astype(bf16)
        return links.burst(
            xr.at[h],
            [
                (xs.at[h, :, lax.rem(x + k, NX)], xr.at[h, k - 1], dict(dx=k))
                for k in (2, 1, 3)
            ],
        )

    def score_head(h):
        for n in range(notes):
            q = q_ref[0, n * BLOCK : (n + 1) * BLOCK, head(h)]
            masked = []
            for slot in range(2):
                e = bl_ref[0, slot, n]
                s = dot(q, chosen(kall[h], e), 1, 1) * scale
                allow = patients[n] == ep8[pl.ds(e, 1), :]
                masked.append(jnp.where(allow, s, masked_score))
            top = jnp.max(jnp.maximum(masked[0], masked[1]), axis=1, keepdims=True)
            weight = [jnp.exp(s - top) for s in masked]
            row_sum = jnp.sum(weight[0] + weight[1], axis=1, keepdims=True)
            inverse = 1.0 / row_sum
            prob = [w * inverse for w in weight]
            for slot in range(2):
                probs[h, n, slot] = prob[slot]
            spread_out(pd, h, n, prob[0].astype(bf16), prob[1].astype(bf16))
        dvs[h] = dot(pd[h], g_ref[0, :, head(h)], 0, 0).astype(bf16).reshape(NZ, NY, 32, DH)

    def value_head(h):
        att = dot(pd[h], vall[h][...].reshape(1024, DH), 1, 0).astype(bf16)
        att_ref[0, :, head(h)] = att
        grad = g_ref[0, :, head(h)]
        delta = jnp.sum(grad.astype(f32) * att.astype(f32), axis=1, keepdims=True)
        for n in range(notes):
            rows = slice(n * BLOCK, (n + 1) * BLOCK)
            low = []
            for slot in range(2):
                pg = dot(grad[rows], chosen(vall[h], bl_ref[0, slot, n]), 1, 1)
                low.append((probs[h, n, slot] * (pg - delta[rows])).astype(bf16))
            spread_out(sd, h, n, low[0], low[1])
        dks[h] = dot(sd[h], q_ref[0, :, head(h)], 0, 0).astype(bf16).reshape(NZ, NY, 32, DH)

    def query_head(h):
        qg = dot(sd[h], kall[h][...].reshape(1024, DH), 1, 0) * scale
        qg_ref[0, :, head(h)] = qg.astype(bf16)
    value_sums = Scatter(links, dvs, va1, vb1, vsa, vsb, vfa, vfb, va2, vb2)
    key_sums = Scatter(links, dks, ka1, kb1, ksa, ksb, kfa, kfb, ka2, kb2)
    keys.done_a()
    score_head(0)
    value_sums.first_a()
    keys.done_b()
    score_head(1)
    value_sums.first_b()
    values = Gather(links, vall)
    arrive(z1a)
    own = pz0[z].astype(f32)
    for k in range(NZ - 1):
        own = own + rz0[k].astype(f32)
    v0[z, y] = own.astype(bf16)
    values.first_a()
    arrive(z1b)
    own = pz1[z].astype(f32)
    for k in range(NZ - 1):
        own = own + rz1[k].astype(f32)
    v1[z, y] = own.astype(bf16)
    values.first_b()
    evt[...] = evz[...].reshape(128, 1024).T
    value_sums.second_a(whole=True)
    value_sums.second_b()
    arrive(values.a1)
    values.second_a()
    values.second_b()
    lz1[z] = value_sums.done_b().astype(bf16)
    low1 = links.burst(lz1.at[pl.ds(0, 3)], [(lz1.at[z], lz1.at[z], to) for to in Z_PEERS])
    lz0[...] = value_sums.done_a(whole=True).astype(bf16)
    c10 = share_head(0)
    x10 = sum_head(0, c10)
    values.done_a()
    value_head(0)
    key_sums.first_a()
    arrive(low1)
    c11 = share_head(1)
    x11 = sum_head(1, c11)
    values.done_b()
    value_head(1)
    key_sums.first_b()
    hand(att_ref, att_out)
    for h, copies in ((0, x10), (1, x11)):
        arrive(copies)
        total = xs[h, :, x].astype(f32)
        for k in range(NX - 1):
            total = total + xr[h, k].astype(f32)
        ys[:, :, head(h)] = total.astype(bf16)
    y1 = links.burst(
        yr, [(ys.at[lax.rem(y + k, NY)], yr.at[k - 1], dict(dy=k)) for k in Y_STEPS]
    )
    for h in range(2):
        query_head(h)
    hand(qg_ref, qg_out)
    arrive(y1)
    total = ys[y].astype(f32)
    for k in range(NY - 1):
        total = total + yr[k].astype(f32)
    sh2[...] = total.astype(bf16)
    far = links.push(sh2, rzh, dzh=1)
    low_rows = jnp.concatenate([lz0[...].reshape(128, DH), lz1[...].reshape(128, DH)], axis=1)
    egs[...] = dot(low_rows, wz[...].reshape(1024, 256), 1, 1).astype(bf16).reshape(NZ, 32, 1024)
    e1 = links.burst(
        egr.at[pl.ds(0, 3)],
        [(egs.at[lax.rem(z + to["dz"], NZ)], egr.at[z], to) for to in Z_PEERS],
    )
    egr[z] = egs[z]
    key_sums.second_a()
    far.wait_recv()
    sh3[...] = sh2[...].astype(f32) + rzh[...].astype(f32)
    mine = pl.ds(pl.multiple_of(part * 16, 16), 16)
    x2 = links.burst(r2.at[pl.ds(0, 112)], [(sh3, r2.at[mine], to) for to in XC_PEERS])
    r2[mine] = sh3[...]
    key_sums.second_b()
    arrive(e1)
    for k in range(NZ):
        hand(egr.at[k], eg_out.at[0, :, k * 1024 : (k + 1) * 1024])
    kg_ref[0, :, head(0)] = (key_sums.done_a() * scale).astype(bf16)
    kg_ref[0, :, head(1)] = (key_sums.done_b() * scale).astype(bf16)
    hand(kg_ref, kg_out)
    arrive(x2)
    hand(r2, wg_out)
    for copy in handed:
        copy.wait()
    links.finish()


def scatter_scratch(whole):
    return [
        pltpu.VMEM((NY - 1, NZ, 32, DH), bf16),
        pltpu.VMEM((NZ - 1, NY, 32, DH), bf16),
        pltpu.VMEM((NZ, 32, DH), bf16),
        pltpu.VMEM((NY, 32, DH), bf16),
        pltpu.VMEM((NZ, 32, DH), f32),
        pltpu.VMEM((NY, 32, DH), f32),
        pltpu.VMEM((NZ - 1, NZ, 32, DH) if whole else (NZ - 1, 32, DH), bf16),
        pltpu.VMEM((NY - 1, 32, DH), bf16),
    ]


def hand_over(*refs):
    held, sem = refs[10:15], refs[15]
    inward = [pltpu.make_async_copy(refs[i], held[i], sem.at[i]) for i in range(5)]
    outward = [pltpu.make_async_copy(held[i], refs[5 + i], sem.at[5 + i]) for i in range(5)]
    for copy in inward:
        copy.start()
    for i in range(5):
        inward[i].wait()
        outward[i].start()
    for copy in outward:
        copy.wait()


def shards(*args):
    def shape(s, t):
        return jax.ShapeDtypeStruct(s, t)

    pair = pltpu.VMEM((2, NZ, NY, 32, DH), bf16)
    single = pltpu.VMEM((NZ, NY, 32, DH), bf16)
    results = pl.pallas_call(
        kernel,
        out_shape=(
            shape((1, 512, 256), bf16),
            shape((1, 512, 256), bf16),
            shape((1, 32, 256), bf16),
            shape((1, 32, 4096), bf16),
            shape((128, 256), f32),
        ),
        in_specs=[pl.BlockSpec(memory_space=pl.ANY)] * 8,
        out_specs=(pl.BlockSpec(memory_space=pl.ANY),) * 5,
        scratch_shapes=[single] * 4
        + [pair] * 2
        + [
            pltpu.VMEM((NX, 2, NY, 16, 256), bf16),
            pltpu.VMEM((NY, 128, 256), bf16),
            pltpu.VMEM((NZ, 32, 1024), bf16),
            pltpu.VMEM((NZ, 32, DH), bf16),
            pltpu.VMEM((NZ, 32, DH), bf16),
            pltpu.VMEM((NZ - 1, 32, DH), bf16),
            pltpu.VMEM((NZ - 1, 32, DH), bf16),
            pltpu.VMEM((1024, 128), bf16),
            pltpu.VMEM((NZ, 32, 1024), bf16),
            pltpu.VMEM((NZ, 32, 1024), bf16),
            pltpu.VMEM((8, BLOCK), jnp.int32),
            pltpu.VMEM((2, 4, 2, BLOCK, BLOCK), f32),
            pltpu.VMEM((2, 512, 1024), bf16),
            pltpu.VMEM((2, 512, 1024), bf16),
            pltpu.VMEM((NZ, 32, DH), bf16),
            pltpu.VMEM((NZ, 32, DH), bf16),
            pltpu.VMEM((2, NY, NX, 2, 16, DH), bf16),
            pltpu.VMEM((2, NY, NX, 16, DH), bf16),
            pltpu.VMEM((2, NY, NX, 16, DH), bf16),
            pltpu.VMEM((2, NX - 1, NY, 16, DH), bf16),
            pltpu.VMEM((NY, 16, 256), bf16),
            pltpu.VMEM((NY - 1, 16, 256), bf16),
            pltpu.VMEM((16, 256), bf16),
            pltpu.VMEM((16, 256), bf16),
            pltpu.VMEM((16, 256), f32),
            pltpu.VMEM((128, 256), f32),
        ]
        + scatter_scratch(True)
        + scatter_scratch(False)
        + [
            pltpu.VMEM((1, 512, 256), bf16),
            pltpu.VMEM((1, 32, 4096), bf16),
            pltpu.VMEM((1, 512, 256), bf16),
            pltpu.VMEM((1, 512), jnp.int32),
            pltpu.VMEM((1, 1024), jnp.int32),
            pltpu.SMEM((1, 2, 4), jnp.int32),
            pltpu.VMEM((1, 512, 256), bf16),
            pltpu.VMEM((1, 512, 256), bf16),
            pltpu.VMEM((1, 32, 256), bf16),
            pltpu.SemaphoreType.DMA((10,)),
            pltpu.SemaphoreType.DMA((8,)),
        ]
        + [pltpu.SemaphoreType.DMA((36,)), pltpu.SemaphoreType.DMA((36,))],
        compiler_params=pltpu.CompilerParams(
            collective_id=0, has_side_effects=True, vmem_limit_bytes=60 * 1024 * 1024
        ),
        name="notes",
    )(*args[:7], jnp.swapaxes(args[7], 1, 2))
    return pl.pallas_call(
        hand_over,
        out_shape=tuple(shape(r.shape, r.dtype) for r in results),
        in_specs=[pl.BlockSpec(memory_space=pl.ANY)] * 5,
        out_specs=(pl.BlockSpec(memory_space=pl.ANY),) * 5,
        scratch_shapes=[pltpu.VMEM(r.shape, r.dtype) for r in results]
        + [pltpu.SemaphoreType.DMA((10,))],
        compiler_params=pltpu.CompilerParams(vmem_limit_bytes=60 * 1024 * 1024),
        name="hand_over",
    )(*results)


def solution(mesh):
    return jax.shard_map(
        shards,
        mesh=mesh,
        in_specs=(
            P("dp", "blk", None),
            P("dp", "blk", None),
            P("dp", "blk", None),
            P("blk", None),
            P("dp", "blk", None),
            P("dp", "blk"),
            P("dp", None),
            P("dp", "blk", None),
        ),
        out_specs=(
            P("dp", "blk", None),
            P("dp", "blk", None),
            P("dp", "blk", None),
            P("dp", "blk", None),
            P("blk", None),
        ),
        check_vma=False,
    )
```
